128 devices in a mesh: group: 4 (over y), dom: 32 (over z, x, core).
Axes of the slice: x: 4, y: 4, z: 4, core: 2. Of those that a mesh axis runs over, the one named last changes fastest.
Arguments:
- nodes: bfloat16 [262144, 128], P(('group', 'dom')), may hold values from -6 to 6
- mesh_edges: bfloat16 [1572864, 128], P(('group', 'dom')), may hold values from -6 to 6
- contact_edges: bfloat16 [16384, 64, 128], P(('group', 'dom')), may hold values from -6 to 6
- mesh_src: int32 [1572864], P(('group', 'dom')), may hold values from 0 to 2559, as said below
- halo_rows: int32 [256, 256], P(('group', 'dom')), may hold values from 0 to 2047
- send_rows: int32 [16384, 64], P(('group', 'dom')), may hold values from 0 to 2047
- partner_rows: int32 [16384, 64], P(('group', 'dom')), may hold values from 0 to 2047
- contact_counts: int32 [128, 128], replicated, may hold values from 1 to 64, as said below
- edge_first: bfloat16 [384, 128], replicated, may hold values from -0.3125 to 0.3125
- edge_second: bfloat16 [128, 128], replicated, may hold values from -0.5 to 0.5
- edge_third: bfloat16 [128, 128], replicated, may hold values from -0.5 to 0.5
- contact_first: bfloat16 [384, 128], replicated, may hold values from -0.3125 to 0.3125
- contact_second: bfloat16 [128, 128], replicated, may hold values from -0.5 to 0.5
- contact_third: bfloat16 [128, 128], replicated, may hold values from -0.5 to 0.5
- node_first: bfloat16 [384, 128], replicated, may hold values from -0.3125 to 0.3125
- node_second: bfloat16 [128, 128], replicated, may hold values from -0.5 to 0.5
- node_third: bfloat16 [128, 128], replicated, may hold values from -0.5 to 0.5
Outputs:
- new_nodes: bfloat16 [262144, 128], P(('group', 'dom'))
- new_mesh_edges: bfloat16 [1572864, 128], P(('group', 'dom'))
- new_contact_edges: bfloat16 [16384, 64, 128], P(('group', 'dom'))
The draws below stay inside these ranges and needn't reach their ends.
Inputs may be any that keep to these rules, and one draw needn't show every extreme that they name: `mesh_src`: the source of device d's edge k (target node n = k // 6) lies in table rows 128 * (n // 128) to 128 * (n // 128) + 128 + 2 * 256 - 1. `contact_counts`: every device sends exactly 64 to some device, and some device receives exactly 64 from every device.
All inputs are finite; a program needn't handle non-finite values.
Results may differ from the reference program's by a relative error of at most 0.0058.
Values may be sent and summed in bfloat16 or wider, within the bound.
No kernel may reach another device: no remote copies, remote signals or barrier semaphores. Data moves between devices by JAX's collectives and lax.ppermute only.
A program may use at most 128 MiB of HBM per device.

```python
import jax
import jax.numpy as jnp
from jax import lax

W = 128
NODE_DEV = 2048
HALO = 256
CAP = 64
BLOCK = 128
EDGE_DEV = 12288
NODES = 262144
N_GROUP = 4
N_DOM = 32
DEVICES = 128


def draw_mesh_src(key, part):
    key = jax.random.fold_in(key, 11)
    total_rows = DEVICES * EDGE_DEV
    local_edge = jnp.arange(total_rows, dtype=jnp.int32) % EDGE_DEV
    target_node = local_edge // 6
    window_start = target_node // BLOCK * BLOCK
    offset = jax.random.randint(key, (total_rows,), 0, BLOCK + 2 * HALO, dtype=jnp.int32)
    return (window_start + offset).astype(jnp.int32)


def draw_contact_counts(key, part):
    key = jax.random.fold_in(key, 23)
    key_base, key_row, key_column = jax.random.split(key, 3)
    counts = jax.random.randint(key_base, (DEVICES, DEVICES), 3 * CAP // 4, CAP + 1, dtype=jnp.int32)
    counts = jnp.minimum(counts, CAP)
    columns = jnp.arange(DEVICES, dtype=jnp.int32)[None, :]
    hot_each = jax.random.randint(key_row, (DEVICES, 1), 0, DEVICES, dtype=jnp.int32)
    counts = jnp.where(columns == hot_each, CAP, counts)
    hot_receiver = jax.random.randint(key_column, (), 0, DEVICES, dtype=jnp.int32)
    counts = jnp.where(columns == hot_receiver, CAP, counts)
    return counts.astype(jnp.int32)


def touch_ends(values, stream_key, least, top_value):
    longest = values.shape.index(max(values.shape))
    spots = []
    for shift in (0, 1):
        where = [jax.random.randint(jax.random.fold_in(stream_key, axis), (), 0, length) for axis, length in enumerate(values.shape)]
        where[longest] = (where[longest] + shift) % values.shape[longest]
        spots.append(tuple(where))
    return values.at[spots[0]].set(least).at[spots[1]].set(top_value)


def levels(rng, dims, pieces, smallest, high):
    level = 1.0
    for axis_at, blocks in pieces:
        heights = jax.random.uniform(jax.random.fold_in(jax.random.fold_in(rng, 6), axis_at), (blocks,), jnp.float32, smallest / len(pieces), high / len(pieces))
        level = level * jnp.repeat(jnp.exp(heights), dims[axis_at] // blocks).reshape((-1,) + (1,) * (len(dims) - 1 - axis_at))
    return level


def normal_values(rng, dims, deviation, limit, shards=(), kind=jnp.bfloat16):
    factor_of = levels(rng, dims, shards, -0.22, 0.18) if shards else 1.0
    result = jax.random.normal(rng, dims, jnp.float32) * deviation * factor_of
    return jnp.minimum(jnp.maximum(result, -limit), limit).astype(kind)


def setup_inputs(seed: int = 0) -> dict:
    arg_keys = jax.random.split(jax.random.key(seed), 18)
    return {
        "nodes": normal_values(arg_keys[0], (NODES, W), 1.0, 6.0, ((0, 128),)),
        "mesh_edges": normal_values(arg_keys[1], (DEVICES * EDGE_DEV, W), 1.0, 6.0, ((0, 128),)),
        "contact_edges": normal_values(arg_keys[2], (DEVICES * DEVICES, CAP, W), 1.0, 6.0, ((0, 128),)),
        "mesh_src": draw_mesh_src(jax.random.fold_in(arg_keys[17], 71), 0),
        "halo_rows": touch_ends(jax.random.randint(arg_keys[4], (2 * DEVICES, HALO), 0, NODE_DEV), jax.random.fold_in(arg_keys[4], 1), 0, NODE_DEV - 1).astype(jnp.int32),
        "send_rows": touch_ends(jax.random.randint(arg_keys[5], (DEVICES * DEVICES, CAP), 0, NODE_DEV), jax.random.fold_in(arg_keys[5], 1), 0, NODE_DEV - 1).astype(jnp.int32),
        "partner_rows": touch_ends(jax.random.randint(arg_keys[6], (DEVICES * DEVICES, CAP), 0, NODE_DEV), jax.random.fold_in(arg_keys[6], 1), 0, NODE_DEV - 1).astype(jnp.int32),
        "contact_counts": draw_contact_counts(jax.random.fold_in(arg_keys[17], 71), 0),
        "edge_first": normal_values(arg_keys[8], (3 * W, W), (3 * W) ** -0.5, 0.3125),
        "edge_second": normal_values(arg_keys[9], (W, W), W ** -0.5, 0.5),
        "edge_third": normal_values(arg_keys[10], (W, W), W ** -0.5, 0.5),
        "contact_first": normal_values(arg_keys[11], (3 * W, W), (3 * W) ** -0.5, 0.3125),
        "contact_second": normal_values(arg_keys[12], (W, W), W ** -0.5, 0.5),
        "contact_third": normal_values(arg_keys[13], (W, W), W ** -0.5, 0.5),
        "node_first": normal_values(arg_keys[14], (3 * W, W), (3 * W) ** -0.5, 0.3125),
        "node_second": normal_values(arg_keys[15], (W, W), W ** -0.5, 0.5),
        "node_third": normal_values(arg_keys[16], (W, W), W ** -0.5, 0.5),
    }


def perceptron(members, first, second, third):
    feature_span = members[0].shape[-1]
    summed = jnp.zeros((members[0].shape[0], first.shape[1]), jnp.float32)
    for position, member in enumerate(members):
        summed = summed + jnp.dot(member, first[position * feature_span:(position + 1) * feature_span], preferred_element_type=jnp.float32)
    hidden_one = jax.nn.relu(summed).astype(jnp.bfloat16)
    hidden_two = jax.nn.relu(jnp.dot(hidden_one, second, preferred_element_type=jnp.float32)).astype(jnp.bfloat16)
    output = jnp.dot(hidden_two, third, preferred_element_type=jnp.float32)
    centred = output - lax.optimization_barrier(jnp.mean(output, axis=-1, keepdims=True))
    return centred * lax.rsqrt(lax.optimization_barrier(jnp.mean(centred * centred, axis=-1, keepdims=True)) + 1e-05)

def take_rows(node_block, row_list):
    return jnp.take(node_block, row_list, axis=0)

def sum_rows(values, row_list):
    return jax.ops.segment_sum(values.astype(jnp.float32), row_list, num_segments=NODE_DEV)

def reference(nodes, mesh_edges, contact_edges, mesh_src, halo_rows, send_rows, partner_rows, contact_counts, edge_first, edge_second, edge_third, contact_first, contact_second, contact_third, node_first, node_second, node_third):
    node_blocks = nodes.reshape(DEVICES, NODE_DEV, W)
    rims = jax.vmap(take_rows)(node_blocks, halo_rows.reshape(DEVICES, 2 * HALO))
    rims = rims.reshape(N_GROUP, N_DOM, 2, HALO, W)
    empty = jnp.zeros((N_GROUP, 1, HALO, W), nodes.dtype)
    lower = jnp.concatenate([empty, rims[:, :-1, 1]], axis=1).reshape(DEVICES, HALO, W)
    upper = jnp.concatenate([rims[:, 1:, 0], empty], axis=1).reshape(DEVICES, HALO, W)
    tables = jnp.concatenate([lower, node_blocks, upper], axis=1)

    def mesh_device(packed):
        node_block, table, edge_block, sources = packed
        source_latent = take_rows(table, sources)
        target_latent = jnp.repeat(node_block, 6, axis=0)
        update = perceptron((edge_block, source_latent, target_latent), edge_first, edge_second, edge_third)
        new_block = (edge_block.astype(jnp.float32) + update).astype(jnp.bfloat16)
        mesh_total = lax.optimization_barrier(jnp.sum(new_block.astype(jnp.float32).reshape(NODE_DEV, 6, W), axis=1)).astype(jnp.bfloat16)
        return (new_block, mesh_total)
    new_mesh, mesh_totals = lax.map(mesh_device, (node_blocks, tables, mesh_edges.reshape(DEVICES, EDGE_DEV, W), mesh_src.reshape(DEVICES, EDGE_DEV)))
    sends = send_rows.reshape(DEVICES, DEVICES * CAP)
    partners = partner_rows.reshape(DEVICES, DEVICES, CAP)
    outgoing = jax.vmap(take_rows)(node_blocks, sends).reshape(DEVICES, DEVICES, CAP, W)
    arrived = jnp.swapaxes(outgoing, 0, 1)
    slot_index = jnp.arange(CAP, dtype=jnp.int32)
    valid_in = slot_index[None, None, :] < jnp.swapaxes(contact_counts, 0, 1)[:, :, None]

    def contact_device(packed):
        node_block, arrivals, partner_list, edge_block, validity = packed
        flat_edges = edge_block.reshape(DEVICES * CAP, W)
        partner_flat = partner_list.reshape(DEVICES * CAP)
        partner_latent = take_rows(node_block, partner_flat)
        update = perceptron((flat_edges, arrivals.reshape(DEVICES * CAP, W), partner_latent), contact_first, contact_second, contact_third)
        updated = (flat_edges.astype(jnp.float32) + update).astype(jnp.bfloat16)
        validity = validity.reshape(DEVICES * CAP, 1)
        kept = jnp.where(validity, updated, flat_edges)
        message = jnp.where(validity, updated, jnp.zeros_like(updated))
        return (kept, message, sum_rows(message, partner_flat))
    kept, messages, received_total = lax.map(contact_device, (node_blocks, arrived, partners, contact_edges.reshape(DEVICES, DEVICES, CAP, W), valid_in))
    returned = jnp.swapaxes(messages.reshape(DEVICES, DEVICES, CAP, W), 0, 1).reshape(DEVICES, DEVICES * CAP, W)
    returned_total = jax.vmap(sum_rows)(returned, sends)
    world_totals = (received_total + returned_total).astype(jnp.bfloat16)

    def node_device(packed):
        node_block, mesh_total, world_total = packed
        update = perceptron((node_block, mesh_total, world_total), node_first, node_second, node_third)
        return (node_block.astype(jnp.float32) + update).astype(jnp.bfloat16)
    new_nodes = lax.map(node_device, (node_blocks, mesh_totals, world_totals))
    return (new_nodes.reshape(NODES, W), new_mesh.reshape(DEVICES * EDGE_DEV, W), kept.reshape(DEVICES * DEVICES, CAP, W))
```

```python
import functools

import jax
import jax.numpy as jnp
from jax import lax
from jax.experimental import pallas as pl
from jax.experimental.pallas import tpu as pltpu
from jax.sharding import PartitionSpec as P

W = 128
BLOCK = 128
HALO = 256
SPLIT = 2
F32 = jnp.float32
BF16 = jnp.bfloat16
ANY = pl.BlockSpec(memory_space=pl.ANY)


def dot(a, b):
    return jnp.dot(a, b, preferred_element_type=F32)


def params(mib=60):
    return pltpu.CompilerParams(vmem_limit_bytes=mib << 20)


def whole(shape):
    return pl.BlockSpec(shape, lambda i: (0,) * len(shape))


def pair(x):
    half = x.shape[0] // 2
    return jnp.concatenate([x[:half], x[half:]], axis=1)


def unpair(x):
    return jnp.concatenate([x[:, :W], x[:, W:]], axis=0)


def twice(w):
    zero = jnp.zeros_like(w)
    return jnp.concatenate(
        [jnp.concatenate([w, zero], axis=1), jnp.concatenate([zero, w], axis=1)], axis=0
    )


def centre(w):
    wide = w.astype(F32)
    wide = wide - jnp.mean(wide, axis=1, keepdims=True)
    high = wide.astype(BF16)
    return high, (wide - high.astype(F32)).astype(BF16)


def fill(weights_ref, second, third):
    weights_ref[0] = twice(second)
    high, low = centre(third)
    weights_ref[1] = twice(high)
    weights_ref[2] = twice(low)
    weights_ref[3] = twice(jnp.full((W, W), 1.0 / W, BF16))


def tail(summed, weights_ref):
    one = jnp.maximum(summed, 0.0).astype(BF16)
    two = jnp.maximum(dot(one, weights_ref[0]), 0.0).astype(BF16)
    centred = dot(two, weights_ref[1]) + dot(two, weights_ref[2])
    variance = dot((centred * centred).astype(BF16), weights_ref[3])
    return centred * lax.rsqrt(variance + 1e-05)


def columns(rows):
    count, length = rows.shape
    return jnp.concatenate(
        [jnp.broadcast_to(rows[i : i + 1], (W, length)).T for i in range(count)], axis=0
    )


def columns_down(rows_ref, peers):
    rows = rows_ref[...]
    steps = rows.shape[1] // peers
    if steps > 1:
        rows = pltpu.roll(rows, (steps - pl.program_id(0)) % steps * peers, 1)
    return jnp.concatenate(
        [jnp.broadcast_to(rows[:, i : i + 1], (rows.shape[0], W)) for i in range(peers)], axis=0
    )


def one_hot(column, span):
    lane = lax.broadcasted_iota(jnp.int32, (column.shape[0], W), 1).astype(jnp.int16)
    short = column.astype(jnp.int16)
    one, zero = jnp.ones((), BF16), jnp.zeros((), BF16)
    return jnp.concatenate(
        [
            jnp.where(short == lane + jnp.int16(first), one, zero)
            for first in range(0, span, W)
        ],
        axis=1,
    )


def one_hot_down(row, first, height):
    index = lax.broadcasted_iota(jnp.int32, (height, row.shape[1]), 0) + first
    wide = jnp.broadcast_to(row, index.shape)
    return jnp.where(
        wide.astype(jnp.int16) == index.astype(jnp.int16), jnp.ones((), BF16), jnp.zeros((), BF16)
    )


def picked(column, nodes_ref, split=SPLIT):
    span = nodes_ref.shape[0] // split
    table = jnp.concatenate([nodes_ref[r * span : (r + 1) * span] for r in range(split)], axis=1)
    result = dot(one_hot(column & (span - 1), span), table)
    part = column >> (span.bit_length() - 1)
    out = result[:, :W]
    for r in range(1, split):
        out = jnp.where(part == r, result[:, r * W : (r + 1) * W], out)
    return out.astype(BF16)


def gather_kernel(peers, rows_ref, nodes_ref, out_ref):
    out_ref[...] = picked(columns_down(rows_ref, peers), nodes_ref)


def gather_rows(rows, nodes, peers):
    length, count = rows.shape
    return pl.pallas_call(
        functools.partial(gather_kernel, peers),
        grid=(count // peers,),
        in_specs=[whole(rows.shape), whole(nodes.shape)],
        out_specs=pl.BlockSpec((peers * length, W), lambda i: (i, 0)),
        out_shape=jax.ShapeDtypeStruct((count * length, W), BF16),
        compiler_params=params(),
        cost_estimate=pl.CostEstimate(
            flops=2 * count * length * nodes.shape[0] * W,
            bytes_accessed=count * length * W * 2,
            transcendentals=0,
        ),
    )(rows, nodes)


def rim_kernel(rows_ref, nodes_ref, out_ref):
    out_ref[...] = picked(columns(rows_ref[...]), nodes_ref)


def rim_rows(rows, nodes):
    return pl.pallas_call(
        rim_kernel,
        out_shape=jax.ShapeDtypeStruct((rows.size, W), BF16),
        compiler_params=params(),
        cost_estimate=pl.CostEstimate(
            flops=2 * rows.size * nodes.shape[0] * W,
            bytes_accessed=(rows.size + nodes.shape[0]) * W * 2,
            transcendentals=0,
        ),
    )(rows, nodes)


def partner_kernel(peers, rows_ref, nodes_ref, edges_ref, first_ref, out_ref):
    latent = picked(columns_down(rows_ref, peers), nodes_ref)
    weights = jnp.concatenate([first_ref[:W], first_ref[2 * W :]], axis=0)
    out_ref[...] = dot(jnp.concatenate([edges_ref[...], latent], axis=1), weights)


def partner_part(rows, nodes, edges, first, peers):
    length, count = rows.shape
    return pl.pallas_call(
        functools.partial(partner_kernel, peers),
        grid=(count // peers,),
        in_specs=[
            whole(rows.shape),
            whole(nodes.shape),
            pl.BlockSpec((peers * length, W), lambda i: (i, 0)),
            whole(first.shape),
        ],
        out_specs=pl.BlockSpec((peers * length, W), lambda i: (i, 0)),
        out_shape=jax.ShapeDtypeStruct((count * length, W), F32),
        compiler_params=params(),
        cost_estimate=pl.CostEstimate(
            flops=2 * count * length * (nodes.shape[0] + 2 * W) * W,
            bytes_accessed=count * length * W * 8,
            transcendentals=0,
        ),
    )(rows, nodes, edges, first)


def contact_kernel(
    capacity, counts_ref, arrived_ref, part_ref, edges_ref, first_ref, second_ref, third_ref,
    after_ref, new_ref, message_ref, entry_ref, weights_ref,
):
    @pl.when(pl.program_id(0) == 0)
    def prepare():
        entry_ref[...] = twice(first_ref[W : 2 * W])
        fill(weights_ref, second_ref[...], third_ref[...])

    rows = arrived_ref.shape[0]
    peers = rows // capacity
    summed = pair(part_ref[...]) + dot(pair(arrived_ref[...]), entry_ref[...])
    update = unpair(tail(summed, weights_ref))
    slot = lax.broadcasted_iota(jnp.int32, (capacity, W), 0)
    for p in range(peers):
        span = slice(p * capacity, (p + 1) * capacity)
        valid = slot < counts_ref[pl.program_id(0) * peers + p]
        old = edges_ref[span].astype(F32)
        new = old + update[span]
        new_ref[span] = jnp.where(valid, new, old).astype(BF16)
        message_ref[span] = jnp.where(valid, new, 0.0).astype(BF16)


def contact_rest(counts, arrived, part, edges, first, second, third, after, rows, capacity):
    total = arrived.shape[0]
    block = pl.BlockSpec((rows, W), lambda i, counts: (i, 0))

    def full(x):
        return pl.BlockSpec(x.shape, lambda i, counts: (0, 0))

    return pl.pallas_call(
        functools.partial(contact_kernel, capacity),
        grid_spec=pltpu.PrefetchScalarGridSpec(
            num_scalar_prefetch=1,
            grid=(total // rows,),
            in_specs=[block, block, block, full(first), full(second), full(third), ANY],
            out_specs=[block, block],
            scratch_shapes=[
                pltpu.VMEM((2 * W, 2 * W), BF16),
                pltpu.VMEM((4, 2 * W, 2 * W), BF16),
            ],
        ),
        out_shape=[jax.ShapeDtypeStruct((total, W), BF16)] * 2,
        compiler_params=params(),
        cost_estimate=pl.CostEstimate(
            flops=2 * total * 4 * W * W, bytes_accessed=total * W * 12, transcendentals=total * W
        ),
    )(counts, arrived, part, edges, first, second, third, after)


def add_messages(rows_ref, values_ref, total_ref, split=SPLIT):
    span = total_ref.shape[0]
    rows = rows_ref[...]
    shift = span.bit_length() - 1
    values = values_ref[...]
    part = columns(rows >> shift).astype(jnp.int16)
    zero = jnp.zeros((), BF16)
    wide = jnp.concatenate(
        [jnp.where(part == jnp.int16(r), values, zero) for r in range(split)], axis=1
    )
    low = rows & (span - 1)
    height = 256
    for first in range(0, span, height):
        hot = jnp.concatenate(
            [one_hot_down(low[i : i + 1], first, height) for i in range(rows.shape[0])], axis=1
        )
        total_ref[first : first + height] += dot(hot, wide)


def received_kernel(rows_ref, values_ref, total_ref):
    @pl.when(pl.program_id(0) == 0)
    def clear():
        total_ref[...] = jnp.zeros_like(total_ref)

    add_messages(rows_ref, values_ref, total_ref)


def received_sum(rows, values, node_count, step):
    shape = (node_count // SPLIT, SPLIT * W)
    return pl.pallas_call(
        received_kernel,
        grid=(rows.shape[0] // step,),
        in_specs=[
            pl.BlockSpec((step, W), lambda i: (i, 0)),
            pl.BlockSpec((step * W, W), lambda i: (i, 0)),
        ],
        out_specs=whole(shape),
        out_shape=jax.ShapeDtypeStruct(shape, F32),
        compiler_params=params(),
        cost_estimate=pl.CostEstimate(
            flops=2 * values.shape[0] * node_count * W,
            bytes_accessed=values.size * 2,
            transcendentals=0,
        ),
    )(rows, values)


def node_kernel(
    rows_ref, values_ref, received_ref, nodes_ref, mesh_ref, first_ref, second_ref, third_ref,
    out_ref, total_ref, weights_ref,
):
    @pl.when(pl.program_id(0) == 0)
    def clear():
        total_ref[...] = received_ref[...]

    add_messages(rows_ref, values_ref, total_ref)

    @pl.when(pl.program_id(0) == pl.num_programs(0) - 1)
    def finish():
        span = total_ref.shape[0]
        world = total_ref[...].astype(BF16)
        nodes = nodes_ref[...]
        mesh = mesh_ref[...]
        summed = dot(pair(nodes), twice(first_ref[:W]))
        summed += dot(pair(mesh), twice(first_ref[W : 2 * W]))
        summed += dot(world, twice(first_ref[2 * W :]))
        fill(weights_ref, second_ref[...], third_ref[...])
        update = tail(summed, weights_ref)
        out_ref[:span] = (nodes[:span].astype(F32) + update[:, :W]).astype(BF16)
        out_ref[span:] = (nodes[span:].astype(F32) + update[:, W:]).astype(BF16)


def node_update(rows, values, received, nodes, mesh_total, first, second, third, step):
    return pl.pallas_call(
        node_kernel,
        grid=(rows.shape[0] // step,),
        in_specs=[
            pl.BlockSpec((step, W), lambda i: (i, 0)),
            pl.BlockSpec((step * W, W), lambda i: (i, 0)),
            whole(received.shape),
            whole(nodes.shape),
            whole(mesh_total.shape),
            whole(first.shape),
            whole(second.shape),
            whole(third.shape),
        ],
        out_specs=whole(nodes.shape),
        out_shape=jax.ShapeDtypeStruct(nodes.shape, BF16),
        scratch_shapes=[
            pltpu.VMEM(received.shape, F32),
            pltpu.VMEM((4, 2 * W, 2 * W), BF16),
        ],
        compiler_params=params(),
        cost_estimate=pl.CostEstimate(
            flops=2 * values.shape[0] * nodes.shape[0] * W,
            bytes_accessed=values.size * 2 + nodes.size * 8,
            transcendentals=nodes.size,
        ),
    )(rows, values, received, nodes, mesh_total, first, second, third)


def mesh_block(degree, block, table_ref, offset, source_ref, edges_ref, first_ref, weights_ref):
    seam = HALO
    span = BLOCK + 2 * seam
    base_row = pl.multiple_of(block * BLOCK, BLOCK)
    edges_here = degree * BLOCK
    window = table_ref[pl.ds(pl.multiple_of(base_row - offset, BLOCK), span)]
    own = table_ref[pl.ds(pl.multiple_of(base_row - offset + seam, BLOCK), BLOCK)]
    table = jnp.concatenate(
        [
            jnp.concatenate([window, jnp.zeros_like(window)], axis=1),
            jnp.concatenate([jnp.zeros_like(own), own], axis=1),
        ],
        axis=0,
    )
    source = one_hot(columns(source_ref[0] - base_row), span)
    edge_row = lax.broadcasted_iota(jnp.int32, (edges_here, W), 0)
    base = lax.broadcasted_iota(jnp.int32, (edges_here, W), 1) * degree
    near = (edge_row >= base) & (edge_row < base + degree)
    target = jnp.where(near, 1.0, 0.0).astype(BF16)
    latent = dot(jnp.concatenate([source, target], axis=1), table).astype(BF16)
    edges = edges_ref[...]
    summed = dot(jnp.concatenate([edges, latent], axis=1), first_ref[...])
    update = unpair(tail(pair(summed), weights_ref))
    new = (edges.astype(F32) + update).astype(BF16)
    down = lax.broadcasted_iota(jnp.int32, (BLOCK, edges_here), 0) * degree
    across = lax.broadcasted_iota(jnp.int32, (BLOCK, edges_here), 1)
    hold = jnp.where((across >= down) & (across < down + degree), 1.0, 0.0).astype(BF16)
    return new, dot(hold, new).astype(BF16)


def inner_kernel(
    degree, place, source_ref, edges_ref, nodes_ref, first_ref, second_ref, third_ref, new_ref,
    total_ref, weights_ref,
):
    @pl.when(pl.program_id(0) == 0)
    def prepare():
        fill(weights_ref, second_ref[...], third_ref[...])

    new_ref[...], total_ref[...] = mesh_block(
        degree, place(pl.program_id(0)), nodes_ref, HALO, source_ref, edges_ref, first_ref,
        weights_ref,
    )


def outer_kernel(
    degree, place, source_ref, edges_ref, nodes_ref, first_ref, second_ref, third_ref, lower_ref,
    upper_ref, mesh_ref, sums_ref, after_ref, new_ref, total_ref, weights_ref, table_ref,
):
    count = nodes_ref.shape[0]

    @pl.when(pl.program_id(0) == 0)
    def prepare():
        fill(weights_ref, second_ref[...], third_ref[...])
        table_ref[:HALO] = lower_ref[...]
        table_ref[HALO : HALO + count] = nodes_ref[...]
        table_ref[HALO + count :] = upper_ref[...]

    new_ref[...], total_ref[...] = mesh_block(
        degree, place(pl.program_id(0)), table_ref, 0, source_ref, edges_ref, first_ref,
        weights_ref,
    )


def mesh_update(kernel, place, steps, source, edges, nodes, weights, extra=(), alias=False):
    degree = edges.shape[0] // nodes.shape[0]
    here = degree * BLOCK
    scratch = [pltpu.VMEM((4, 2 * W, 2 * W), BF16)]
    extra_specs = []
    if alias:
        scratch.append(pltpu.VMEM((nodes.shape[0] + 2 * HALO, W), BF16))
        extra_specs = [whole(extra[0].shape), whole(extra[1].shape), ANY, ANY, ANY]
    return pl.pallas_call(
        functools.partial(kernel, degree, place),
        grid=(steps,),
        in_specs=[
            pl.BlockSpec((1, degree, BLOCK), lambda i: (place(i), 0, 0)),
            pl.BlockSpec((here, W), lambda i: (place(i), 0)),
            whole(nodes.shape),
        ]
        + [whole(w.shape) for w in weights]
        + extra_specs,
        out_specs=[
            pl.BlockSpec((here, W), lambda i: (place(i), 0)),
            pl.BlockSpec((BLOCK, W), lambda i: (place(i), 0)),
        ],
        out_shape=[
            jax.ShapeDtypeStruct(edges.shape, BF16),
            jax.ShapeDtypeStruct(nodes.shape, BF16),
        ],
        scratch_shapes=scratch,
        input_output_aliases={8: 0, 9: 1} if alias else {},
        compiler_params=params(),
        cost_estimate=pl.CostEstimate(
            flops=2 * steps * here * 1800 * W,
            bytes_accessed=steps * here * W * 4,
            transcendentals=steps * here * W,
        ),
    )(source, edges, nodes, *weights, *extra)


def shards(
    nodes,
    mesh_edges,
    contact_edges,
    mesh_src,
    halo_rows,
    send_rows,
    partner_rows,
    contact_counts,
    edge_first,
    edge_second,
    edge_third,
    contact_first,
    contact_second,
    contact_third,
    node_first,
    node_second,
    node_third,
):
    axes = ("group", "dom")
    node_count = nodes.shape[0]
    degree = mesh_edges.shape[0] // node_count
    peers, capacity = send_rows.shape
    slots = peers * capacity

    outgoing = gather_rows(send_rows.T, nodes, 32).reshape(peers, capacity, W)
    arrived = lax.all_to_all(outgoing, axes, split_axis=0, concat_axis=0, tiled=True)

    edges = contact_edges.reshape(slots, W)
    part = partner_part(partner_rows.T, nodes, edges, contact_first, 32)
    blocks = node_count // BLOCK
    edge_blocks = HALO // BLOCK
    source = mesh_src.reshape(blocks, degree, BLOCK)
    edge_weights = (edge_first, edge_second, edge_third)
    inner_mesh, inner_total = mesh_update(
        inner_kernel, lambda i: i + edge_blocks, blocks - 2 * edge_blocks, source, mesh_edges,
        nodes, edge_weights,
    )

    size = lax.axis_size("dom")
    device = lax.axis_index("group") * size + lax.axis_index("dom")
    counts = lax.dynamic_index_in_dim(contact_counts, device, 1, keepdims=False)
    new_contacts, message = contact_rest(
        counts, arrived.reshape(slots, W), part, edges, contact_first, contact_second,
        contact_third, inner_total, 1024, capacity,
    )
    returned = lax.all_to_all(
        message.reshape(peers, capacity, W), axes, split_axis=0, concat_axis=0, tiled=True
    ).reshape(slots, W)

    rims = rim_rows(halo_rows.reshape(-1, W), nodes)
    lower = lax.ppermute(rims[HALO:], "dom", [(i, i + 1) for i in range(size - 1)])
    upper = lax.ppermute(rims[:HALO], "dom", [(i + 1, i) for i in range(size - 1)])
    new_mesh, mesh_total = mesh_update(
        outer_kernel,
        lambda i: jnp.where(i < edge_blocks, i, i + blocks - 2 * edge_blocks),
        2 * edge_blocks, source, mesh_edges, nodes, edge_weights,
        (lower, upper, inner_mesh, inner_total, message), True,
    )
    received = received_sum(partner_rows.reshape(-1, W), message, node_count, 16)
    new_nodes = node_update(
        send_rows.reshape(-1, W), returned, received, nodes, mesh_total, node_first, node_second,
        node_third, 16,
    )
    return (new_nodes, new_mesh, new_contacts.reshape(peers, capacity, W))


def solution(mesh):
    split = P(("group", "dom"))
    in_specs = (split,) * 7 + (P(),) * 10
    return jax.shard_map(
        shards, mesh=mesh, in_specs=in_specs, out_specs=(split,) * 3, check_vma=False
    )
```

```python
import functools

import jax
import jax.numpy as jnp
from jax import lax
from jax.experimental import pallas as pl
from jax.experimental.pallas import tpu as pltpu
from jax.sharding import PartitionSpec as P

W = 128
BLOCK = 128
HALO = 256
SPLIT = 2
F32 = jnp.float32
BF16 = jnp.bfloat16
ANY = pl.BlockSpec(memory_space=pl.ANY)
VMEM = pl.BlockSpec(memory_space=pltpu.VMEM)
HBM = pl.BlockSpec(memory_space=pltpu.HBM)
SMEM = pl.BlockSpec(memory_space=pltpu.SMEM)


def dot(a, b):
    return jnp.dot(a, b, preferred_element_type=F32)


def params(mib=60):
    return pltpu.CompilerParams(vmem_limit_bytes=mib << 20)


def cost(flops, moved, transcendentals=0):
    return pl.CostEstimate(flops=flops, bytes_accessed=moved, transcendentals=transcendentals)


def shape(rows, dtype=BF16, width=W):
    return jax.ShapeDtypeStruct((rows, width), dtype)


def pipeline(stages, count):
    held = {}
    for step in range(count + len(stages) - 1):
        given = {}
        for s, stage in enumerate(stages):
            chunk = step - s
            if 0 <= chunk < count:
                given[s] = stage(chunk, held.get(s - 1))
        held = given


def cut(chunk, size):
    return slice(chunk * size, (chunk + 1) * size)


def pair(x):
    half = x.shape[0] // 2
    return jnp.concatenate([x[:half], x[half:]], axis=1)


def unpair(x):
    return jnp.concatenate([x[:, :W], x[:, W:]], axis=0)


def twice(w):
    zero = jnp.zeros_like(w)
    return jnp.concatenate(
        [jnp.concatenate([w, zero], axis=1), jnp.concatenate([zero, w], axis=1)], axis=0
    )


def fill(weights_ref, second, third):
    wide = third.astype(F32)
    wide = wide - jnp.mean(wide, axis=1, keepdims=True)
    high = wide.astype(BF16)
    weights_ref[0] = twice(second)
    weights_ref[1] = twice(high)
    weights_ref[2] = twice((wide - high.astype(F32)).astype(BF16))
    weights_ref[3] = twice(jnp.full((W, W), 1.0 / W, BF16))


def network(weights_ref):
    def second(chunk, summed):
        return dot(jnp.maximum(summed, 0.0).astype(BF16), weights_ref[0])

    def third(chunk, summed):
        two = jnp.maximum(summed, 0.0).astype(BF16)
        return dot(two, weights_ref[1]) + dot(two, weights_ref[2])

    def spread(chunk, centred):
        return centred, dot((centred * centred).astype(BF16), weights_ref[3])

    return [second, third, spread]


def normal(given):
    centred, variance = given
    return centred * lax.rsqrt(variance + 1e-05)


def columns(rows):
    count, length = rows.shape
    return jnp.concatenate(
        [jnp.broadcast_to(rows[i : i + 1], (W, length)).T for i in range(count)], axis=0
    )


def columns_down(rows):
    length, count = rows.shape
    return jnp.concatenate(
        [jnp.broadcast_to(rows[:, i : i + 1], (length, W)) for i in range(count)], axis=0
    )


def one_hot(column, span):
    lane = lax.broadcasted_iota(jnp.int32, (column.shape[0], W), 1).astype(jnp.int16)
    short = column.astype(jnp.int16)
    one, zero = jnp.ones((), BF16), jnp.zeros((), BF16)
    return jnp.concatenate(
        [
            jnp.where(short == lane + jnp.int16(first), one, zero)
            for first in range(0, span, W)
        ],
        axis=1,
    )


def picking(column, nodes_ref, use):
    span = nodes_ref.shape[0] // SPLIT
    table = jnp.concatenate([nodes_ref[cut(r, span)] for r in range(SPLIT)], axis=1)

    def select(chunk, unused):
        numbers = column(chunk)
        return one_hot(numbers & (span - 1), span), numbers >> (span.bit_length() - 1)

    def multiply(chunk, given):
        hot, part = given
        result = dot(hot, table)
        out = result[:, :W]
        for r in range(1, SPLIT):
            out = jnp.where(part == r, result[:, r * W : (r + 1) * W], out)
        return use(chunk, out.astype(BF16))

    return [select, multiply]


def gather_kernel(rows_ref, nodes_ref, out_ref, rows_buf, nodes_buf, out_buf, sem):
    fetch_rows = pltpu.make_async_copy(rows_ref, rows_buf, sem.at[0])
    fetch_nodes = pltpu.make_async_copy(nodes_ref, nodes_buf, sem.at[1])
    fetch_rows.start()
    fetch_nodes.start()
    fetch_rows.wait()
    fetch_nodes.wait()
    peers = 8
    length, count = rows_buf.shape
    size = peers * length

    def use(chunk, rows):
        out_buf[cut(chunk, size)] = rows
        pltpu.make_async_copy(
            out_buf.at[cut(chunk, size)], out_ref.at[cut(chunk, size)], sem.at[2]
        ).start()

    def column(chunk):
        return columns_down(rows_buf[:, cut(chunk, peers)])

    pipeline(picking(column, nodes_buf, use), count // peers)
    pltpu.make_async_copy(out_buf, out_ref, sem.at[2]).wait()


def gather_rows(rows, nodes):
    total = rows.size
    return pl.pallas_call(
        gather_kernel,
        in_specs=[HBM, HBM],
        out_specs=HBM,
        out_shape=shape(total),
        scratch_shapes=[
            pltpu.VMEM(rows.shape, rows.dtype),
            pltpu.VMEM(nodes.shape, BF16),
            pltpu.VMEM((total, W), BF16),
            pltpu.SemaphoreType.DMA((3,)),
        ],
        compiler_params=params(),
        cost_estimate=cost(2 * total * nodes.shape[0] * W, total * W * 2),
    )(rows, nodes)


def rim_kernel(rows_ref, nodes_ref, first_ref, last_ref):
    lists = HALO // W
    outs = (first_ref, last_ref)

    def use(chunk, rows):
        outs[chunk][...] = rows

    def column(chunk):
        return columns(rows_ref[cut(chunk, lists)])

    pipeline(picking(column, nodes_ref, use), len(outs))


def rim_rows(rows, nodes):
    return pl.pallas_call(
        rim_kernel,
        in_specs=[VMEM, VMEM],
        out_specs=[VMEM, VMEM],
        out_shape=[shape(HALO)] * 2,
        compiler_params=params(),
        cost_estimate=cost(2 * rows.size * nodes.shape[0] * W, (rows.size + nodes.shape[0]) * 256),
    )(rows, nodes)


def partner_kernel(
    rows_ref, nodes_ref, edges_ref, first_ref, second_ref, third_ref, out_ref, prepared_ref,
    out_buf, weights_ref, sem,
):
    fill(weights_ref, second_ref[...], third_ref[...])
    weights_ref[4] = twice(first_ref[W : 2 * W])
    weights = jnp.concatenate([first_ref[:W], first_ref[2 * W :]], axis=0)
    peers = 8
    length, count = rows_ref.shape
    size = peers * length

    def column(chunk):
        return columns_down(rows_ref[:, cut(chunk, peers)])

    def add(chunk, latent):
        here = cut(chunk, size)
        out_buf[here] = dot(jnp.concatenate([edges_ref[here], latent], axis=1), weights)
        pltpu.make_async_copy(out_buf.at[here], out_ref.at[here], sem.at[0]).start()

    keep = pltpu.make_async_copy(
        weights_ref, prepared_ref.at[: weights_ref.shape[0]], sem.at[1]
    )
    keep.start()
    pipeline(picking(column, nodes_ref, lambda chunk, rows: rows) + [add], count // peers)
    keep.wait()
    pltpu.make_async_copy(out_buf, out_ref, sem.at[0]).wait()


def partner_part(rows, nodes, edges, first, second, third):
    total = rows.size
    return pl.pallas_call(
        partner_kernel,
        in_specs=[VMEM] * 6,
        out_specs=[HBM, HBM],
        out_shape=[shape(total, F32), jax.ShapeDtypeStruct((96, 2 * W, 2 * W), BF16)],
        scratch_shapes=[
            pltpu.VMEM((total, W), F32),
            pltpu.VMEM((5, 2 * W, 2 * W), BF16),
            pltpu.SemaphoreType.DMA((2,)),
        ],
        compiler_params=params(),
        cost_estimate=cost(2 * total * (nodes.shape[0] + 2 * W) * W, total * W * 8),
    )(rows, nodes, edges, first, second, third)


class Fetch:
    def __init__(self, source, target, sem, parts=1):
        self.rows = source.shape[0] // parts
        self.copies = [
            pltpu.make_async_copy(
                source.at[cut(i, self.rows)], target.at[cut(i, self.rows)], sem.at[i]
            )
            for i in range(parts)
        ]
        self.ready = 0

    def start(self, i=0):
        self.copies[i].start()

    def until(self, rows):
        while self.ready < len(self.copies) and self.ready * self.rows < rows:
            self.copies[self.ready].wait()
            self.ready += 1


def contact_kernel(
    capacity, counts_ref, arrived_ref, part_hbm, edges_hbm, weights_hbm, lower_ref, upper_ref,
    after_ref, new_ref, message_ref, part_ref, edges_ref, weights_ref, new_buf, sem, in_sem,
):
    size = 512
    peers = size // capacity
    parts = 8
    slot = lax.broadcasted_iota(jnp.int32, (capacity, W), 0)
    weights = Fetch(weights_hbm.at[: weights_ref.shape[0]], weights_ref, in_sem.at[2])
    part = Fetch(part_hbm, part_ref, in_sem.at[0], parts)
    edges = Fetch(edges_hbm, edges_ref, in_sem.at[1], parts)
    weights.start()
    for i in range(parts):
        part.start(i)
        edges.start(i)
    weights.until(1)

    def first(chunk, unused):
        for fetch in (part, edges):
            fetch.until((chunk + 1) * size)
        came = pair(arrived_ref[cut(chunk, size)])
        return dot(came, weights_ref[4]) + pair(part_ref[cut(chunk, size)])

    def finish(chunk, given):
        here = cut(chunk, size)
        old = edges_ref[here].astype(F32)
        new = old + unpair(normal(given))
        kept, sent = [], []
        for p in range(peers):
            valid = slot < counts_ref[chunk * peers + p]
            one = new[cut(p, capacity)]
            kept.append(jnp.where(valid, one, old[cut(p, capacity)]))
            sent.append(jnp.where(valid, one, 0.0))
        message_ref[here] = jnp.concatenate(sent, axis=0).astype(BF16)
        new_buf[here] = jnp.concatenate(kept, axis=0).astype(BF16)
        pltpu.make_async_copy(new_buf.at[here], new_ref.at[here], sem.at[0]).start()

    pipeline([first] + network(weights_ref) + [finish], arrived_ref.shape[0] // size)
    pltpu.make_async_copy(new_buf, new_ref, sem.at[0]).wait()


def contact_rest(counts, arrived, part, edges, weights, lower, upper, after, capacity):
    total = arrived.shape[0]
    return pl.pallas_call(
        functools.partial(contact_kernel, capacity),
        in_specs=[SMEM, VMEM, HBM, HBM, HBM, ANY, ANY, ANY],
        out_specs=[HBM, VMEM],
        out_shape=[shape(total)] * 2,
        scratch_shapes=[
            pltpu.VMEM((total, W), F32),
            pltpu.VMEM((total, W), BF16),
            pltpu.VMEM((5, 2 * W, 2 * W), BF16),
            pltpu.VMEM((total, W), BF16),
            pltpu.SemaphoreType.DMA((1,)),
            pltpu.SemaphoreType.DMA((3, 8)),
        ],
        compiler_params=params(48),
        cost_estimate=cost(2 * total * 4 * W * W, total * W * 14, total * W),
    )(counts, arrived, part, edges, weights, lower, upper, after)


def adding(rows_ref, values_ref, total_ref, need=lambda rows: None):
    span = total_ref.shape[0]
    shift = span.bit_length() - 1
    lists = 8
    height = 256
    zero, one = jnp.zeros((), BF16), jnp.ones((), BF16)
    index = lax.broadcasted_iota(jnp.int32, (height, W), 0).astype(jnp.int16)

    def select(chunk, unused):
        need((chunk + 1) * lists * W)
        rows = rows_ref[cut(chunk, lists)]
        values = values_ref[cut(chunk, lists * W)]
        part = columns(rows >> shift).astype(jnp.int16)
        wide = jnp.concatenate(
            [jnp.where(part == jnp.int16(r), values, zero) for r in range(SPLIT)], axis=1
        )
        low = rows & (span - 1)
        across = [
            jnp.concatenate(
                [jnp.broadcast_to(low[i : i + 1], (16, W)).astype(jnp.int16)] * (height // 16),
                axis=0,
            )
            for i in range(lists)
        ]
        hot = [
            jnp.concatenate(
                [jnp.where(row == index + jnp.int16(first), one, zero) for row in across], axis=1
            )
            for first in range(0, span, height)
        ]
        return hot, wide

    def multiply(chunk, given):
        hot, wide = given
        for k, rows in enumerate(hot):
            total_ref[cut(k, height)] += dot(rows, wide)

    return [select, multiply], rows_ref.shape[0] // lists


def received_kernel(
    rows_ref, values_ref, nodes_ref, inner_ref, outer_ref, first_ref, second_ref, third_ref,
    sums_hbm, prepared_hbm, total_ref, part_ref, weights_ref, sem,
):
    total_ref[...] = jnp.zeros_like(total_ref)
    fill(weights_ref, second_ref[...], third_ref[...])
    weights_ref[4] = twice(first_ref[2 * W :])
    edge = outer_ref.shape[0] // 2
    mesh = jnp.concatenate([outer_ref[:edge], inner_ref[...], outer_ref[edge:]], axis=0)
    part_ref[...] = dot(pair(nodes_ref[...]), twice(first_ref[:W])) + dot(
        pair(mesh), twice(first_ref[W : 2 * W])
    )
    span = total_ref.shape[0]
    keep = [
        pltpu.make_async_copy(part_ref, sums_hbm.at[span : 2 * span], sem.at[0]),
        pltpu.make_async_copy(weights_ref, prepared_hbm.at[: weights_ref.shape[0]], sem.at[1]),
    ]
    for copy in keep:
        copy.start()
    pipeline(*adding(rows_ref, values_ref, total_ref))
    keep.append(pltpu.make_async_copy(total_ref, sums_hbm.at[:span], sem.at[2]))
    keep[-1].start()
    for copy in keep:
        copy.wait()


def received_sum(rows, values, nodes, inner, outer, first, second, third):
    span = nodes.shape[0] // SPLIT
    return pl.pallas_call(
        received_kernel,
        in_specs=[VMEM] * 8,
        out_specs=[HBM] * 2,
        out_shape=[
            shape(12 * span, F32, SPLIT * W),
            jax.ShapeDtypeStruct((96, 2 * W, 2 * W), BF16),
        ],
        scratch_shapes=[
            pltpu.VMEM((span, SPLIT * W), F32),
            pltpu.VMEM((span, SPLIT * W), F32),
            pltpu.VMEM((5, 2 * W, 2 * W), BF16),
            pltpu.SemaphoreType.DMA((3,)),
        ],
        compiler_params=params(),
        cost_estimate=cost(2 * values.shape[0] * nodes.shape[0] * W, values.size * 2),
    )(rows, values, nodes, inner, outer, first, second, third)


def node_kernel(
    rows_hbm, values_ref, sums_hbm, prepared_hbm, nodes_ref, out_ref, rows_ref, total_ref,
    part_ref, weights_ref, out_buf, in_sem, sem,
):
    rows = Fetch(rows_hbm, rows_ref, in_sem.at[0])
    later = [
        Fetch(source, target, in_sem.at[1 + i])
        for i, (source, target) in enumerate(
            [
                (sums_hbm.at[: total_ref.shape[0]], total_ref),
                (sums_hbm.at[total_ref.shape[0] : 2 * total_ref.shape[0]], part_ref),
                (prepared_hbm.at[: weights_ref.shape[0]], weights_ref),
            ]
        )
    ]
    rows.start()
    for fetch in later:
        fetch.start()
    rows.until(1)
    later[0].until(1)
    pipeline(*adding(rows_ref, values_ref, total_ref))
    for fetch in later[1:]:
        fetch.until(1)
    span = total_ref.shape[0]
    size = 256

    def first(chunk, unused):
        here = cut(chunk, size)
        return part_ref[here] + dot(total_ref[here].astype(BF16), weights_ref[4])

    def finish(chunk, given):
        update = normal(given)
        for r in range(SPLIT):
            here = slice(r * span + chunk * size, r * span + (chunk + 1) * size)
            new = nodes_ref[here].astype(F32) + update[:, r * W : (r + 1) * W]
            out_buf[here] = new.astype(BF16)
            pltpu.make_async_copy(out_buf.at[here], out_ref.at[here], sem.at[0]).start()

    pipeline([first] + network(weights_ref) + [finish], span // size)
    pltpu.make_async_copy(out_buf, out_ref, sem.at[0]).wait()


def node_update(rows, values, sums, prepared, nodes):
    span = nodes.shape[0] // SPLIT
    return pl.pallas_call(
        node_kernel,
        in_specs=[HBM, VMEM, HBM, HBM, VMEM],
        out_specs=HBM,
        out_shape=shape(nodes.shape[0]),
        scratch_shapes=[
            pltpu.VMEM(rows.shape, rows.dtype),
            pltpu.VMEM((span, SPLIT * W), F32),
            pltpu.VMEM((span, SPLIT * W), F32),
            pltpu.VMEM((5, 2 * W, 2 * W), BF16),
            pltpu.VMEM(nodes.shape, BF16),
            pltpu.SemaphoreType.DMA((4, 1)),
            pltpu.SemaphoreType.DMA((1,)),
        ],
        compiler_params=params(48),
        cost_estimate=cost(2 * values.shape[0] * nodes.shape[0] * W, values.size * 4, nodes.size),
    )(rows, values, sums, prepared, nodes)


def mesh_stages(
    degree, blocks, table_ref, offset, source_ref, edges_ref, first_ref, weights_ref, target_ref,
    new_buf, new_ref, total_ref, sem,
):
    span = BLOCK + 2 * HALO
    here = degree * BLOCK
    edge_row = lax.broadcasted_iota(jnp.int32, (here, W), 0)
    base = lax.broadcasted_iota(jnp.int32, (here, W), 1) * degree
    near = (edge_row >= base) & (edge_row < base + degree)
    target_ref[...] = jnp.where(near, 1.0, 0.0).astype(BF16)
    down = lax.broadcasted_iota(jnp.int32, (BLOCK, here), 0) * degree
    across = lax.broadcasted_iota(jnp.int32, (BLOCK, here), 1)
    hold = jnp.where((across >= down) & (across < down + degree), 1.0, 0.0).astype(BF16)

    def select(chunk, unused):
        row = blocks[chunk] * BLOCK
        return one_hot(columns(source_ref[blocks[chunk]] - row), span)

    def latents(chunk, hot):
        row = blocks[chunk] * BLOCK - offset
        window = table_ref[row : row + span]
        own = table_ref[row + HALO : row + HALO + BLOCK]
        table = jnp.concatenate(
            [
                jnp.concatenate([window, jnp.zeros_like(window)], axis=1),
                jnp.concatenate([jnp.zeros_like(own), own], axis=1),
            ],
            axis=0,
        )
        return dot(jnp.concatenate([hot, target_ref[...]], axis=1), table).astype(BF16)

    def first(chunk, latent):
        edges = edges_ref[cut(blocks[chunk], here)]
        return pair(dot(jnp.concatenate([edges, latent], axis=1), first_ref[...]))

    def finish(chunk, given):
        edges = edges_ref[cut(blocks[chunk], here)]
        new = (edges.astype(F32) + unpair(normal(given))).astype(BF16)
        new_buf[cut(chunk, here)] = new
        pltpu.make_async_copy(
            new_buf.at[cut(chunk, here)], new_ref.at[cut(blocks[chunk], here)], sem
        ).start()
        return new

    def gather(chunk, new):
        total_ref[cut(chunk, BLOCK)] = dot(hold, new).astype(BF16)

    pipeline([select, latents, first] + network(weights_ref) + [finish, gather], len(blocks))
    pltpu.make_async_copy(new_buf, new_ref.at[: len(blocks) * here], sem).wait()


def inner_kernel(
    degree, blocks, source_ref, edges_ref, nodes_ref, first_ref, second_ref, third_ref, after_ref,
    new_ref, total_ref, token_ref, weights_ref, target_ref, new_buf, sem,
):
    token_ref[...] = jnp.zeros_like(token_ref)
    fill(weights_ref, second_ref[...], third_ref[...])
    mesh_stages(
        degree, blocks, nodes_ref, HALO, source_ref, edges_ref, first_ref, weights_ref, target_ref,
        new_buf, new_ref, total_ref, sem.at[0],
    )


def outer_kernel(
    degree, blocks, source_ref, edges_ref, nodes_ref, first_ref, second_ref, third_ref, after_ref,
    lower_ref, upper_ref, mesh_ref, new_ref, total_ref, weights_ref, target_ref, new_buf, sem,
    table_ref,
):
    count = nodes_ref.shape[0]
    fill(weights_ref, second_ref[...], third_ref[...])
    table_ref[:HALO] = lower_ref[...]
    table_ref[HALO : HALO + count] = nodes_ref[...]
    table_ref[HALO + count :] = upper_ref[...]
    mesh_stages(
        degree, blocks, table_ref, 0, source_ref, edges_ref, first_ref, weights_ref, target_ref,
        new_buf, new_ref, total_ref, sem.at[0],
    )


def mesh_update(kernel, blocks, source, edges, nodes, weights, after, extra=()):
    degree = edges.shape[0] // nodes.shape[0]
    here = degree * BLOCK
    rows = len(blocks) * here
    scratch = [
        pltpu.VMEM((4, 2 * W, 2 * W), BF16),
        pltpu.VMEM((here, W), BF16),
        pltpu.VMEM((rows, W), BF16),
        pltpu.SemaphoreType.DMA((1,)),
    ]
    if extra:
        scratch.append(pltpu.VMEM((nodes.shape[0] + 2 * HALO, W), BF16))
    return pl.pallas_call(
        functools.partial(kernel, degree, blocks),
        in_specs=[VMEM] * 6 + [ANY] + ([VMEM, VMEM, ANY] if extra else []),
        out_specs=[ANY, VMEM] + ([] if extra else [VMEM]),
        out_shape=[shape(edges.shape[0]), shape(len(blocks) * BLOCK)]
        + ([] if extra else [shape(16)]),
        scratch_shapes=scratch,
        input_output_aliases={9: 0} if extra else {},
        compiler_params=params(),
        cost_estimate=cost(2 * rows * 1800 * W, rows * W * 4, rows * W),
    )(source, edges, nodes, *weights, after, *extra)


def shards(
    nodes,
    mesh_edges,
    contact_edges,
    mesh_src,
    halo_rows,
    send_rows,
    partner_rows,
    contact_counts,
    edge_first,
    edge_second,
    edge_third,
    contact_first,
    contact_second,
    contact_third,
    node_first,
    node_second,
    node_third,
):
    axes = ("group", "dom")
    node_count = nodes.shape[0]
    degree = mesh_edges.shape[0] // node_count
    peers, capacity = send_rows.shape
    slots = peers * capacity

    outgoing = gather_rows(send_rows.T, nodes).reshape(peers, capacity, W)
    arrived = lax.all_to_all(outgoing, axes, split_axis=0, concat_axis=0, tiled=True)

    size = lax.axis_size("dom")
    to_lower, to_upper = rim_rows(halo_rows.reshape(-1, W), nodes)
    lower = lax.ppermute(to_upper, "dom", [(i, i + 1) for i in range(size - 1)])
    upper = lax.ppermute(to_lower, "dom", [(i + 1, i) for i in range(size - 1)])

    edges = contact_edges.reshape(slots, W)
    part, contact_weights = partner_part(
        partner_rows.T, nodes, edges, contact_first, contact_second, contact_third
    )
    blocks = node_count // BLOCK
    late = 2 * HALO // BLOCK
    inside = tuple(range(late, blocks - late))
    outside = tuple(range(late)) + tuple(range(blocks - late, blocks))
    source = mesh_src.reshape(blocks, degree, BLOCK)
    edge_weights = (edge_first, edge_second, edge_third)
    new_mesh, inner_total, token = mesh_update(
        inner_kernel, inside, source, mesh_edges, nodes, edge_weights, to_lower
    )

    device = lax.axis_index("group") * size + lax.axis_index("dom")
    counts = lax.dynamic_index_in_dim(contact_counts, device, 1, keepdims=False)
    new_contacts, message = contact_rest(
        counts, arrived.reshape(slots, W), part, edges, contact_weights, lower, upper,
        token, capacity
    )
    returned = lax.all_to_all(
        message.reshape(peers, capacity, W), axes, split_axis=0, concat_axis=0, tiled=True
    ).reshape(slots, W)

    new_mesh, outer_total = mesh_update(
        outer_kernel, outside, source, mesh_edges, nodes, edge_weights, message,
        (lower, upper, new_mesh),
    )
    sums, prepared = received_sum(
        partner_rows.reshape(-1, W), message, nodes, inner_total, outer_total, node_first,
        node_second, node_third,
    )
    new_nodes = node_update(
        send_rows.reshape(-1, W), returned, sums, prepared, nodes
    )
    return (new_nodes, new_mesh, new_contacts.reshape(peers, capacity, W))


def solution(mesh):
    split = P(("group", "dom"))
    in_specs = (split,) * 7 + (P(),) * 10
    return jax.shard_map(
        shards, mesh=mesh, in_specs=in_specs, out_specs=(split,) * 3, check_vma=False
    )
```

```python
import functools

import jax
import jax.numpy as jnp
from jax import lax
from jax.experimental import pallas as pl
from jax.experimental.pallas import tpu as pltpu
from jax.sharding import PartitionSpec as P

W = 128
BLOCK = 128
HALO = 256
SPLIT = 2
F32 = jnp.float32
BF16 = jnp.bfloat16
ANY = pl.BlockSpec(memory_space=pl.ANY)
VMEM = pl.BlockSpec(memory_space=pltpu.VMEM)
HBM = pl.BlockSpec(memory_space=pltpu.HBM)
SMEM = pl.BlockSpec(memory_space=pltpu.SMEM)


def dot(a, b):
    return jnp.dot(a, b, preferred_element_type=F32)


def params(mib=60):
    return pltpu.CompilerParams(vmem_limit_bytes=mib << 20)


def cost(flops, moved, transcendentals=0):
    return pl.CostEstimate(flops=flops, bytes_accessed=moved, transcendentals=transcendentals)


def shape(rows, dtype=BF16, width=W):
    return jax.ShapeDtypeStruct((rows, width), dtype)


def pipeline(stages, count):
    held = {}
    for step in range(count + len(stages) - 1):
        given = {}
        for s, stage in enumerate(stages):
            chunk = step - s
            if 0 <= chunk < count:
                given[s] = stage(chunk, held.get(s - 1))
        held = given


def cut(chunk, size):
    return slice(chunk * size, (chunk + 1) * size)


def pair(x):
    half = x.shape[0] // 2
    return jnp.concatenate([x[:half], x[half:]], axis=1)


def unpair(x):
    return jnp.concatenate([x[:, :W], x[:, W:]], axis=0)


def twice(w):
    zero = jnp.zeros_like(w)
    return jnp.concatenate(
        [jnp.concatenate([w, zero], axis=1), jnp.concatenate([zero, w], axis=1)], axis=0
    )


def fill(weights_ref, second, third):
    wide = third.astype(F32)
    wide = wide - jnp.mean(wide, axis=1, keepdims=True)
    high = wide.astype(BF16)
    weights_ref[0] = twice(second)
    weights_ref[1] = twice(high)
    weights_ref[2] = twice((wide - high.astype(F32)).astype(BF16))
    weights_ref[3] = twice(jnp.full((W, W), 1.0 / W, BF16))


def network(weights_ref):
    def second(chunk, summed):
        return dot(jnp.maximum(summed, 0.0).astype(BF16), weights_ref[0])

    def third(chunk, summed):
        two = jnp.maximum(summed, 0.0).astype(BF16)
        return dot(two, weights_ref[1]) + dot(two, weights_ref[2])

    def spread(chunk, centred):
        return centred, dot((centred * centred).astype(BF16), weights_ref[3])

    return [second, third, spread]


def normal(given):
    centred, variance = given
    return centred * lax.rsqrt(variance + 1e-05)


def columns(rows):
    count, length = rows.shape
    return jnp.concatenate(
        [jnp.broadcast_to(rows[i : i + 1], (W, length)).T for i in range(count)], axis=0
    )


def columns_down(rows):
    length, count = rows.shape
    return jnp.concatenate(
        [jnp.broadcast_to(rows[:, i : i + 1], (length, W)) for i in range(count)], axis=0
    )


def one_hot(column, span):
    lane = lax.broadcasted_iota(jnp.int32, (column.shape[0], W), 1).astype(jnp.int16)
    short = column.astype(jnp.int16)
    one, zero = jnp.ones((), BF16), jnp.zeros((), BF16)
    return jnp.concatenate(
        [
            jnp.where(short == lane + jnp.int16(first), one, zero)
            for first in range(0, span, W)
        ],
        axis=1,
    )


def picking(column, nodes_ref, use):
    span = nodes_ref.shape[0] // SPLIT
    table = jnp.concatenate([nodes_ref[cut(r, span)] for r in range(SPLIT)], axis=1)

    def select(chunk, unused):
        numbers = column(chunk)
        return one_hot(numbers & (span - 1), span), numbers >> (span.bit_length() - 1)

    def multiply(chunk, given):
        hot, part = given
        result = dot(hot, table)
        out = result[:, :W]
        for r in range(1, SPLIT):
            out = jnp.where(part == r, result[:, r * W : (r + 1) * W], out)
        return use(chunk, out.astype(BF16))

    return [select, multiply]


def gather_kernel(rows_ref, nodes_ref, out_ref, rows_buf, nodes_buf, out_buf, sem):
    fetch_rows = pltpu.make_async_copy(rows_ref, rows_buf, sem.at[0])
    fetch_nodes = pltpu.make_async_copy(nodes_ref, nodes_buf, sem.at[1])
    fetch_rows.start()
    fetch_nodes.start()
    fetch_rows.wait()
    fetch_nodes.wait()
    peers = 8
    length, count = rows_buf.shape
    size = peers * length

    def use(chunk, rows):
        out_buf[cut(chunk, size)] = rows
        pltpu.make_async_copy(
            out_buf.at[cut(chunk, size)], out_ref.at[cut(chunk, size)], sem.at[2]
        ).start()

    def column(chunk):
        return columns_down(rows_buf[:, cut(chunk, peers)])

    pipeline(picking(column, nodes_buf, use), count // peers)
    pltpu.make_async_copy(out_buf, out_ref, sem.at[2]).wait()


def gather_rows(rows, nodes):
    total = rows.size
    return pl.pallas_call(
        gather_kernel,
        in_specs=[HBM, HBM],
        out_specs=HBM,
        out_shape=shape(total),
        scratch_shapes=[
            pltpu.VMEM(rows.shape, rows.dtype),
            pltpu.VMEM(nodes.shape, BF16),
            pltpu.VMEM((total, W), BF16),
            pltpu.SemaphoreType.DMA((3,)),
        ],
        compiler_params=params(),
        cost_estimate=cost(2 * total * nodes.shape[0] * W, total * W * 2),
    )(rows, nodes)


def rim_kernel(rows_ref, nodes_ref, first_ref, last_ref):
    lists = HALO // W
    outs = (first_ref, last_ref)

    def use(chunk, rows):
        outs[chunk][...] = rows

    def column(chunk):
        return columns(rows_ref[cut(chunk, lists)])

    pipeline(picking(column, nodes_ref, use), len(outs))


def rim_rows(rows, nodes):
    return pl.pallas_call(
        rim_kernel,
        in_specs=[VMEM, VMEM],
        out_specs=[VMEM, VMEM],
        out_shape=[shape(HALO)] * 2,
        compiler_params=params(),
        cost_estimate=cost(2 * rows.size * nodes.shape[0] * W, (rows.size + nodes.shape[0]) * 256),
    )(rows, nodes)


def partner_kernel(
    rows_ref, nodes_ref, edges_ref, first_ref, out_ref, out_buf, sem,
):
    weights = jnp.concatenate([first_ref[:W], first_ref[2 * W :]], axis=0)
    peers = 8
    length, count = rows_ref.shape
    size = peers * length

    def column(chunk):
        return columns_down(rows_ref[:, cut(chunk, peers)])

    def add(chunk, latent):
        here = cut(chunk, size)
        out_buf[here] = dot(jnp.concatenate([edges_ref[here], latent], axis=1), weights)
        pltpu.make_async_copy(out_buf.at[here], out_ref.at[here], sem.at[0]).start()

    pipeline(picking(column, nodes_ref, lambda chunk, rows: rows) + [add], count // peers)
    pltpu.make_async_copy(out_buf, out_ref, sem.at[0]).wait()


def partner_part(rows, nodes, edges, first):
    total = rows.size
    return pl.pallas_call(
        partner_kernel,
        in_specs=[VMEM] * 4,
        out_specs=HBM,
        out_shape=shape(total, F32),
        scratch_shapes=[
            pltpu.VMEM((total, W), F32),
            pltpu.SemaphoreType.DMA((1,)),
        ],
        compiler_params=params(),
        cost_estimate=cost(2 * total * (nodes.shape[0] + 2 * W) * W, total * W * 8),
    )(rows, nodes, edges, first)


class Fetch:
    def __init__(self, source, target, sem, parts=1):
        self.rows = source.shape[0] // parts
        self.copies = [
            pltpu.make_async_copy(
                source.at[cut(i, self.rows)], target.at[cut(i, self.rows)], sem.at[i]
            )
            for i in range(parts)
        ]
        self.ready = 0

    def start(self, i=0):
        self.copies[i].start()

    def until(self, rows):
        while self.ready < len(self.copies) and self.ready * self.rows < rows:
            self.copies[self.ready].wait()
            self.ready += 1


def contact_kernel(
    capacity, counts_ref, arrived_ref, part_hbm, edges_hbm, first_ref, second_ref, third_ref, lower_ref, upper_ref,
    after_ref, message_ref, part_ref, edges_ref, weights_ref, in_sem,
):
    size = 512
    peers = size // capacity
    parts = 2
    slot = lax.broadcasted_iota(jnp.int32, (capacity, W), 0)
    part = Fetch(part_hbm, part_ref, in_sem.at[0], parts)
    edges = Fetch(edges_hbm, edges_ref, in_sem.at[1], parts)
    for i in range(parts):
        part.start(i)
        edges.start(i)
    fill(weights_ref, second_ref[...], third_ref[...])
    weights_ref[4] = twice(first_ref[W : 2 * W])

    def first(chunk, unused):
        for fetch in (part, edges):
            fetch.until((chunk + 1) * size)
        came = pair(arrived_ref[cut(chunk, size)])
        return dot(came, weights_ref[4]) + pair(part_ref[cut(chunk, size)])

    def finish(chunk, given):
        here = cut(chunk, size)
        new = edges_ref[here].astype(F32) + unpair(normal(given))
        sent = [
            jnp.where(slot < counts_ref[chunk * peers + p], new[cut(p, capacity)], 0.0)
            for p in range(peers)
        ]
        message_ref[here] = jnp.concatenate(sent, axis=0).astype(BF16)

    pipeline([first] + network(weights_ref) + [finish], arrived_ref.shape[0] // size)


def contact_rest(counts, arrived, part, edges, weights, lower, upper, after, capacity):
    total = arrived.shape[0]
    return pl.pallas_call(
        functools.partial(contact_kernel, capacity),
        in_specs=[SMEM, VMEM, HBM, HBM, VMEM, VMEM, VMEM, ANY, ANY, ANY],
        out_specs=VMEM,
        out_shape=shape(total),
        scratch_shapes=[
            pltpu.VMEM((total, W), F32),
            pltpu.VMEM((total, W), BF16),
            pltpu.VMEM((5, 2 * W, 2 * W), BF16),
            pltpu.SemaphoreType.DMA((3, 8)),
        ],
        compiler_params=params(48),
        cost_estimate=cost(2 * total * 4 * W * W, total * W * 14, total * W),
    )(counts, arrived, part, edges, *weights, lower, upper, after)


def adding(rows_ref, values_ref, total_ref, also=lambda chunk, values: None):
    span = total_ref.shape[0]
    shift = span.bit_length() - 1
    lists = 8
    height = 256
    zero, one = jnp.zeros((), BF16), jnp.ones((), BF16)
    index = lax.broadcasted_iota(jnp.int32, (height, W), 0).astype(jnp.int16)

    def select(chunk, unused):
        rows = rows_ref[cut(chunk, lists)]
        values = values_ref[cut(chunk, lists * W)]
        also(chunk, values)
        part = columns(rows >> shift).astype(jnp.int16)
        wide = jnp.concatenate(
            [jnp.where(part == jnp.int16(r), values, zero) for r in range(SPLIT)], axis=1
        )
        low = rows & (span - 1)
        across = [
            jnp.concatenate(
                [jnp.broadcast_to(low[i : i + 1], (16, W)).astype(jnp.int16)] * (height // 16),
                axis=0,
            )
            for i in range(lists)
        ]
        hot = [
            jnp.concatenate(
                [jnp.where(row == index + jnp.int16(first), one, zero) for row in across], axis=1
            )
            for first in range(0, span, height)
        ]
        return hot, wide

    def multiply(chunk, given):
        hot, wide = given
        for k, rows in enumerate(hot):
            total_ref[cut(k, height)] += dot(rows, wide)

    return [select, multiply], rows_ref.shape[0] // lists


def received_kernel(
    capacity, counts_ref, edges_ref, rows_ref, values_ref, nodes_ref, inner_ref, outer_ref, first_ref, second_ref, third_ref,
    sums_hbm, prepared_hbm, new_hbm, total_ref, part_ref, weights_ref, new_buf, sem,
):
    total_ref[...] = jnp.zeros_like(total_ref)
    fill(weights_ref, second_ref[...], third_ref[...])
    weights_ref[4] = twice(first_ref[2 * W :])
    edge = outer_ref.shape[0] // 2
    mesh = jnp.concatenate([outer_ref[:edge], inner_ref[...], outer_ref[edge:]], axis=0)
    part_ref[...] = dot(pair(nodes_ref[...]), twice(first_ref[:W])) + dot(
        pair(mesh), twice(first_ref[W : 2 * W])
    )
    span = total_ref.shape[0]
    keep = [
        pltpu.make_async_copy(part_ref, sums_hbm.at[span : 2 * span], sem.at[0]),
        pltpu.make_async_copy(weights_ref, prepared_hbm.at[: weights_ref.shape[0]], sem.at[1]),
    ]
    for copy in keep:
        copy.start()
    slot = lax.broadcasted_iota(jnp.int32, (capacity, W), 0)

    def renew(chunk, values):
        size = values.shape[0]
        here = cut(chunk, size)
        edges = edges_ref[here].astype(F32)
        sent = values.astype(F32)
        peers = size // capacity
        new = [
            jnp.where(
                slot < counts_ref[chunk * peers + p], sent[cut(p, capacity)], edges[cut(p, capacity)]
            )
            for p in range(peers)
        ]
        new_buf[here] = jnp.concatenate(new, axis=0).astype(BF16)
        pltpu.make_async_copy(new_buf.at[here], new_hbm.at[here], sem.at[3]).start()

    pipeline(*adding(rows_ref, values_ref, total_ref, renew))
    keep.append(pltpu.make_async_copy(new_buf, new_hbm, sem.at[3]))
    keep.append(pltpu.make_async_copy(total_ref, sums_hbm.at[:span], sem.at[2]))
    keep[-1].start()
    for copy in keep:
        copy.wait()


def received_sum(
    counts, edges, rows, values, nodes, inner, outer, first, second, third, capacity
):
    span = nodes.shape[0] // SPLIT
    return pl.pallas_call(
        functools.partial(received_kernel, capacity),
        in_specs=[SMEM] + [VMEM] * 9,
        out_specs=[HBM] * 3,
        out_shape=[
            shape(12 * span, F32, SPLIT * W),
            jax.ShapeDtypeStruct((96, 2 * W, 2 * W), BF16),
            shape(values.shape[0]),
        ],
        scratch_shapes=[
            pltpu.VMEM((span, SPLIT * W), F32),
            pltpu.VMEM((span, SPLIT * W), F32),
            pltpu.VMEM((5, 2 * W, 2 * W), BF16),
            pltpu.VMEM(values.shape, BF16),
            pltpu.SemaphoreType.DMA((4,)),
        ],
        compiler_params=params(),
        cost_estimate=cost(2 * values.shape[0] * nodes.shape[0] * W, values.size * 2),
    )(counts, edges, rows, values, nodes, inner, outer, first, second, third)


def node_kernel(
    rows_ref, values_ref, sums_hbm, prepared_hbm, nodes_ref, out_ref, total_ref, sums_ref,
    weights_ref, out_buf, in_sem, sem,
):
    span = total_ref.shape[0]
    sums = Fetch(sums_hbm.at[: 2 * span], sums_ref, in_sem.at[0])
    weights = Fetch(prepared_hbm.at[: weights_ref.shape[0]], weights_ref, in_sem.at[1])
    sums.start()
    weights.start()
    total_ref[...] = jnp.zeros_like(total_ref)
    pipeline(*adding(rows_ref, values_ref, total_ref))
    sums.until(1)
    weights.until(1)
    size = 256

    def first(chunk, unused):
        here = cut(chunk, size)
        world = (total_ref[here] + sums_ref[here]).astype(BF16)
        part = sums_ref[slice(span + chunk * size, span + (chunk + 1) * size)]
        return part + dot(world, weights_ref[4])

    def finish(chunk, given):
        update = normal(given)
        for r in range(SPLIT):
            here = slice(r * span + chunk * size, r * span + (chunk + 1) * size)
            new = nodes_ref[here].astype(F32) + update[:, r * W : (r + 1) * W]
            out_buf[here] = new.astype(BF16)
            pltpu.make_async_copy(out_buf.at[here], out_ref.at[here], sem.at[0]).start()

    pipeline([first] + network(weights_ref) + [finish], span // size)
    pltpu.make_async_copy(out_buf, out_ref, sem.at[0]).wait()


def node_update(rows, values, sums, prepared, nodes):
    span = nodes.shape[0] // SPLIT
    return pl.pallas_call(
        node_kernel,
        in_specs=[VMEM, VMEM, HBM, HBM, VMEM],
        out_specs=HBM,
        out_shape=shape(nodes.shape[0]),
        scratch_shapes=[
            pltpu.VMEM((span, SPLIT * W), F32),
            pltpu.VMEM((2 * span, SPLIT * W), F32),
            pltpu.VMEM((5, 2 * W, 2 * W), BF16),
            pltpu.VMEM(nodes.shape, BF16),
            pltpu.SemaphoreType.DMA((2, 1)),
            pltpu.SemaphoreType.DMA((1,)),
        ],
        compiler_params=params(48),
        cost_estimate=cost(2 * values.shape[0] * nodes.shape[0] * W, values.size * 4, nodes.size),
    )(rows, values, sums, prepared, nodes)


def mesh_stages(
    degree, blocks, table_ref, offset, source_ref, edges_ref, first_ref, weights_ref, target_ref,
    new_buf, new_ref, total_ref, sem,
):
    span = BLOCK + 2 * HALO
    here = degree * BLOCK
    edge_row = lax.broadcasted_iota(jnp.int32, (here, W), 0)
    base = lax.broadcasted_iota(jnp.int32, (here, W), 1) * degree
    near = (edge_row >= base) & (edge_row < base + degree)
    target_ref[...] = jnp.where(near, 1.0, 0.0).astype(BF16)
    down = lax.broadcasted_iota(jnp.int32, (BLOCK, here), 0) * degree
    across = lax.broadcasted_iota(jnp.int32, (BLOCK, here), 1)
    hold = jnp.where((across >= down) & (across < down + degree), 1.0, 0.0).astype(BF16)

    def select(chunk, unused):
        row = blocks[chunk] * BLOCK
        return one_hot(columns(source_ref[blocks[chunk]] - row), span)

    def latents(chunk, hot):
        row = blocks[chunk] * BLOCK - offset
        window = table_ref[row : row + span]
        own = table_ref[row + HALO : row + HALO + BLOCK]
        table = jnp.concatenate(
            [
                jnp.concatenate([window, jnp.zeros_like(window)], axis=1),
                jnp.concatenate([jnp.zeros_like(own), own], axis=1),
            ],
            axis=0,
        )
        return dot(jnp.concatenate([hot, target_ref[...]], axis=1), table).astype(BF16)

    def first(chunk, latent):
        edges = edges_ref[cut(blocks[chunk], here)]
        return pair(dot(jnp.concatenate([edges, latent], axis=1), first_ref[...]))

    def finish(chunk, given):
        edges = edges_ref[cut(blocks[chunk], here)]
        new = (edges.astype(F32) + unpair(normal(given))).astype(BF16)
        new_buf[cut(chunk, here)] = new
        pltpu.make_async_copy(
            new_buf.at[cut(chunk, here)], new_ref.at[cut(blocks[chunk], here)], sem
        ).start()
        return new

    def gather(chunk, new):
        total_ref[cut(chunk, BLOCK)] = dot(hold, new).astype(BF16)

    pipeline([select, latents, first] + network(weights_ref) + [finish, gather], len(blocks))
    pltpu.make_async_copy(new_buf, new_ref.at[: len(blocks) * here], sem).wait()


def inner_kernel(
    degree, blocks, source_ref, edges_ref, nodes_ref, first_ref, second_ref, third_ref, after_ref,
    new_ref, total_ref, token_ref, weights_ref, target_ref, new_buf, sem,
):
    token_ref[...] = jnp.zeros_like(token_ref)
    fill(weights_ref, second_ref[...], third_ref[...])
    mesh_stages(
        degree, blocks, nodes_ref, HALO, source_ref, edges_ref, first_ref, weights_ref, target_ref,
        new_buf, new_ref, total_ref, sem.at[0],
    )


def outer_kernel(
    degree, blocks, source_ref, edges_ref, nodes_ref, first_ref, second_ref, third_ref, after_ref,
    lower_ref, upper_ref, mesh_ref, new_ref, total_ref, weights_ref, target_ref, new_buf, sem,
    table_ref,
):
    count = nodes_ref.shape[0]
    fill(weights_ref, second_ref[...], third_ref[...])
    table_ref[:HALO] = lower_ref[...]
    table_ref[HALO : HALO + count] = nodes_ref[...]
    table_ref[HALO + count :] = upper_ref[...]
    mesh_stages(
        degree, blocks, table_ref, 0, source_ref, edges_ref, first_ref, weights_ref, target_ref,
        new_buf, new_ref, total_ref, sem.at[0],
    )


def mesh_update(kernel, blocks, source, edges, nodes, weights, after, extra=()):
    degree = edges.shape[0] // nodes.shape[0]
    here = degree * BLOCK
    rows = len(blocks) * here
    scratch = [
        pltpu.VMEM((4, 2 * W, 2 * W), BF16),
        pltpu.VMEM((here, W), BF16),
        pltpu.VMEM((rows, W), BF16),
        pltpu.SemaphoreType.DMA((1,)),
    ]
    if extra:
        scratch.append(pltpu.VMEM((nodes.shape[0] + 2 * HALO, W), BF16))
    return pl.pallas_call(
        functools.partial(kernel, degree, blocks),
        in_specs=[VMEM] * 6 + [ANY] + ([VMEM, VMEM, ANY] if extra else []),
        out_specs=[ANY, VMEM] + ([] if extra else [VMEM]),
        out_shape=[shape(edges.shape[0]), shape(len(blocks) * BLOCK)]
        + ([] if extra else [shape(16)]),
        scratch_shapes=scratch,
        input_output_aliases={9: 0} if extra else {},
        compiler_params=params(),
        cost_estimate=cost(2 * rows * 1800 * W, rows * W * 4, rows * W),
    )(source, edges, nodes, *weights, after, *extra)


def shards(
    nodes,
    mesh_edges,
    contact_edges,
    mesh_src,
    halo_rows,
    send_rows,
    partner_rows,
    contact_counts,
    edge_first,
    edge_second,
    edge_third,
    contact_first,
    contact_second,
    contact_third,
    node_first,
    node_second,
    node_third,
):
    axes = ("group", "dom")
    node_count = nodes.shape[0]
    degree = mesh_edges.shape[0] // node_count
    peers, capacity = send_rows.shape
    slots = peers * capacity

    outgoing = gather_rows(send_rows.T, nodes).reshape(peers, capacity, W)
    arrived = lax.all_to_all(outgoing, axes, split_axis=0, concat_axis=0, tiled=True)

    size = lax.axis_size("dom")
    to_lower, to_upper = rim_rows(halo_rows.reshape(-1, W), nodes)
    lower = lax.ppermute(to_upper, "dom", [(i, i + 1) for i in range(size - 1)])
    upper = lax.ppermute(to_lower, "dom", [(i + 1, i) for i in range(size - 1)])

    edges = contact_edges.reshape(slots, W)
    part = partner_part(
        partner_rows.T, nodes, edges, contact_first
    )
    blocks = node_count // BLOCK
    late = 2 * HALO // BLOCK
    inside = tuple(range(late, blocks - late))
    outside = tuple(range(late)) + tuple(range(blocks - late, blocks))
    source = mesh_src.reshape(blocks, degree, BLOCK)
    edge_weights = (edge_first, edge_second, edge_third)
    new_mesh, inner_total, token = mesh_update(
        inner_kernel, inside, source, mesh_edges, nodes, edge_weights, to_lower
    )

    device = lax.axis_index("group") * size + lax.axis_index("dom")
    counts = lax.dynamic_index_in_dim(contact_counts, device, 1, keepdims=False)
    message = contact_rest(
        counts, arrived.reshape(slots, W), part, edges,
        (contact_first, contact_second, contact_third), lower, upper,
        token, capacity
    )
    returned = lax.all_to_all(
        message.reshape(peers, capacity, W), axes, split_axis=0, concat_axis=0, tiled=True
    ).reshape(slots, W)

    new_mesh, outer_total = mesh_update(
        outer_kernel, outside, source, mesh_edges, nodes, edge_weights, message,
        (lower, upper, new_mesh),
    )
    sums, prepared, new_contacts = received_sum(
        counts, edges, partner_rows.reshape(-1, W), message, nodes, inner_total, outer_total,
        node_first, node_second, node_third, capacity,
    )
    new_nodes = node_update(
        send_rows.reshape(-1, W), returned, sums, prepared, nodes
    )
    return (new_nodes, new_mesh, new_contacts.reshape(peers, capacity, W))


def solution(mesh):
    split = P(("group", "dom"))
    in_specs = (split,) * 7 + (P(),) * 10
    return jax.shard_map(
        shards, mesh=mesh, in_specs=in_specs, out_specs=(split,) * 3, check_vma=False
    )
```

```python
import functools

import jax
import jax.numpy as jnp
from jax import lax
from jax.experimental import pallas as pl
from jax.experimental.pallas import tpu as pltpu
from jax.sharding import PartitionSpec as P

W = 128
BLOCK = 128
HALO = 256
SPLIT = 2
F32 = jnp.float32
BF16 = jnp.bfloat16
ANY = pl.BlockSpec(memory_space=pl.ANY)
VMEM = pl.BlockSpec(memory_space=pltpu.VMEM)
HBM = pl.BlockSpec(memory_space=pltpu.HBM)
SMEM = pl.BlockSpec(memory_space=pltpu.SMEM)


def dot(a, b):
    return jnp.dot(a, b, preferred_element_type=F32)


def params(mib=60):
    return pltpu.CompilerParams(vmem_limit_bytes=mib << 20)


def cost(flops, moved, transcendentals=0):
    return pl.CostEstimate(flops=flops, bytes_accessed=moved, transcendentals=transcendentals)


def shape(rows, dtype=BF16, width=W):
    return jax.ShapeDtypeStruct((rows, width), dtype)


def pipeline(stages, count):
    held = {}
    for step in range(count + len(stages) - 1):
        given = {}
        for s, stage in enumerate(stages):
            chunk = step - s
            if 0 <= chunk < count:
                given[s] = stage(chunk, held.get(s - 1))
        held = given


def cut(chunk, size):
    return slice(chunk * size, (chunk + 1) * size)


def pair(x):
    half = x.shape[0] // 2
    return jnp.concatenate([x[:half], x[half:]], axis=1)


def unpair(x):
    return jnp.concatenate([x[:, :W], x[:, W:]], axis=0)


def twice(w):
    zero = jnp.zeros_like(w)
    return jnp.concatenate(
        [jnp.concatenate([w, zero], axis=1), jnp.concatenate([zero, w], axis=1)], axis=0
    )


def fill(weights_ref, second, third):
    wide = third.astype(F32)
    wide = wide - jnp.mean(wide, axis=1, keepdims=True)
    high = wide.astype(BF16)
    weights_ref[0] = twice(second)
    weights_ref[1] = twice(high)
    weights_ref[2] = twice((wide - high.astype(F32)).astype(BF16))
    weights_ref[3] = twice(jnp.full((W, W), 1.0 / W, BF16))


def network(weights_ref):
    def second(chunk, summed):
        return dot(jnp.maximum(summed, 0.0).astype(BF16), weights_ref[0])

    def third(chunk, summed):
        two = jnp.maximum(summed, 0.0).astype(BF16)
        return dot(two, weights_ref[1]) + dot(two, weights_ref[2])

    def spread(chunk, centred):
        return centred, dot((centred * centred).astype(BF16), weights_ref[3])

    return [second, third, spread]


def normal(given):
    centred, variance = given
    return centred * lax.rsqrt(variance + 1e-05)


def columns(rows):
    count, length = rows.shape
    return jnp.concatenate(
        [jnp.broadcast_to(rows[i : i + 1], (W, length)).T for i in range(count)], axis=0
    )


def columns_down(rows):
    length, count = rows.shape
    return jnp.concatenate(
        [jnp.broadcast_to(rows[:, i : i + 1], (length, W)) for i in range(count)], axis=0
    )


def one_hot(column, span):
    lane = lax.broadcasted_iota(jnp.int32, (column.shape[0], W), 1).astype(jnp.int16)
    short = column.astype(jnp.int16)
    one, zero = jnp.ones((), BF16), jnp.zeros((), BF16)
    return jnp.concatenate(
        [
            jnp.where(short == lane + jnp.int16(first), one, zero)
            for first in range(0, span, W)
        ],
        axis=1,
    )


def picking(column, nodes_ref, use):
    span = nodes_ref.shape[0] // SPLIT
    table = jnp.concatenate([nodes_ref[cut(r, span)] for r in range(SPLIT)], axis=1)

    def select(chunk, unused):
        numbers = column(chunk)
        return one_hot(numbers & (span - 1), span), numbers >> (span.bit_length() - 1)

    def multiply(chunk, given):
        hot, part = given
        result = dot(hot, table)
        out = result[:, :W]
        for r in range(1, SPLIT):
            out = jnp.where(part == r, result[:, r * W : (r + 1) * W], out)
        return use(chunk, out.astype(BF16))

    return [select, multiply]


def gather_kernel(rows_ref, nodes_ref, out_ref, rows_buf, nodes_buf, out_buf, sem):
    fetch_rows = pltpu.make_async_copy(rows_ref, rows_buf, sem.at[0])
    fetch_nodes = pltpu.make_async_copy(nodes_ref, nodes_buf, sem.at[1])
    fetch_rows.start()
    fetch_nodes.start()
    fetch_rows.wait()
    fetch_nodes.wait()
    peers = 8
    length, count = rows_buf.shape
    size = peers * length

    def use(chunk, rows):
        out_buf[cut(chunk, size)] = rows
        pltpu.make_async_copy(
            out_buf.at[cut(chunk, size)], out_ref.at[cut(chunk, size)], sem.at[2]
        ).start()

    def column(chunk):
        return columns_down(rows_buf[:, cut(chunk, peers)])

    pipeline(picking(column, nodes_buf, use), count // peers)
    pltpu.make_async_copy(out_buf, out_ref, sem.at[2]).wait()


def gather_rows(rows, nodes):
    total = rows.size
    return pl.pallas_call(
        gather_kernel,
        in_specs=[HBM, HBM],
        out_specs=HBM,
        out_shape=shape(total),
        scratch_shapes=[
            pltpu.VMEM(rows.shape, rows.dtype),
            pltpu.VMEM(nodes.shape, BF16),
            pltpu.VMEM((total, W), BF16),
            pltpu.SemaphoreType.DMA((3,)),
        ],
        compiler_params=params(),
        cost_estimate=cost(2 * total * nodes.shape[0] * W, total * W * 2),
    )(rows, nodes)


def rim_kernel(rows_ref, nodes_ref, first_ref, last_ref):
    lists = HALO // W
    outs = (first_ref, last_ref)

    def use(chunk, rows):
        outs[chunk][...] = rows

    def column(chunk):
        return columns(rows_ref[cut(chunk, lists)])

    pipeline(picking(column, nodes_ref, use), len(outs))


def rim_rows(rows, nodes):
    return pl.pallas_call(
        rim_kernel,
        in_specs=[VMEM, VMEM],
        out_specs=[VMEM, VMEM],
        out_shape=[shape(HALO)] * 2,
        compiler_params=params(),
        cost_estimate=cost(2 * rows.size * nodes.shape[0] * W, (rows.size + nodes.shape[0]) * 256),
    )(rows, nodes)


def partner_kernel(
    rows_ref, nodes_ref, edges_ref, first_ref, out_ref, out_buf, sem,
):
    weights = jnp.concatenate([first_ref[:W], first_ref[2 * W :]], axis=0)
    peers = 8
    length, count = rows_ref.shape
    size = peers * length

    def column(chunk):
        return columns_down(rows_ref[:, cut(chunk, peers)])

    def add(chunk, latent):
        here = cut(chunk, size)
        out_buf[here] = dot(jnp.concatenate([edges_ref[here], latent], axis=1), weights)
        pltpu.make_async_copy(out_buf.at[here], out_ref.at[here], sem.at[0]).start()

    pipeline(picking(column, nodes_ref, lambda chunk, rows: rows) + [add], count // peers)
    pltpu.make_async_copy(out_buf, out_ref, sem.at[0]).wait()


def partner_part(rows, nodes, edges, first):
    total = rows.size
    return pl.pallas_call(
        partner_kernel,
        in_specs=[VMEM] * 4,
        out_specs=HBM,
        out_shape=shape(total, F32),
        scratch_shapes=[
            pltpu.VMEM((total, W), F32),
            pltpu.SemaphoreType.DMA((1,)),
        ],
        compiler_params=params(),
        cost_estimate=cost(2 * total * (nodes.shape[0] + 2 * W) * W, total * W * 8),
    )(rows, nodes, edges, first)


class Fetch:
    def __init__(self, source, target, sem, parts=1):
        self.rows = source.shape[0] // parts
        self.copies = [
            pltpu.make_async_copy(
                source.at[cut(i, self.rows)], target.at[cut(i, self.rows)], sem.at[i]
            )
            for i in range(parts)
        ]
        self.ready = 0

    def start(self, i=0):
        self.copies[i].start()

    def until(self, rows):
        while self.ready < len(self.copies) and self.ready * self.rows < rows:
            self.copies[self.ready].wait()
            self.ready += 1


def contact_kernel(
    capacity, counts_ref, arrived_ref, part_hbm, edges_hbm, first_ref, second_ref, third_ref, lower_ref, upper_ref,
    after_ref, message_ref, part_ref, edges_ref, weights_ref, in_sem,
):
    size = 512
    peers = size // capacity
    parts = 2
    slot = lax.broadcasted_iota(jnp.int32, (capacity, W), 0)
    part = Fetch(part_hbm, part_ref, in_sem.at[0], parts)
    edges = Fetch(edges_hbm, edges_ref, in_sem.at[1], parts)
    for i in range(parts):
        part.start(i)
    for i in range(parts):
        edges.start(i)
    fill(weights_ref, second_ref[...], third_ref[...])
    weights_ref[4] = twice(first_ref[W : 2 * W])

    def first(chunk, unused):
        part.until((chunk + 1) * size)
        came = pair(arrived_ref[cut(chunk, size)])
        return dot(came, weights_ref[4]) + pair(part_ref[cut(chunk, size)])

    def finish(chunk, given):
        here = cut(chunk, size)
        edges.until((chunk + 1) * size)
        new = edges_ref[here].astype(F32) + unpair(normal(given))
        sent = [
            jnp.where(slot < counts_ref[chunk * peers + p], new[cut(p, capacity)], 0.0)
            for p in range(peers)
        ]
        message_ref[here] = jnp.concatenate(sent, axis=0).astype(BF16)

    pipeline([first] + network(weights_ref) + [finish], arrived_ref.shape[0] // size)


def contact_rest(counts, arrived, part, edges, weights, lower, upper, after, capacity):
    total = arrived.shape[0]
    return pl.pallas_call(
        functools.partial(contact_kernel, capacity),
        in_specs=[SMEM, VMEM, HBM, HBM, VMEM, VMEM, VMEM, ANY, ANY, ANY],
        out_specs=VMEM,
        out_shape=shape(total),
        scratch_shapes=[
            pltpu.VMEM((total, W), F32),
            pltpu.VMEM((total, W), BF16),
            pltpu.VMEM((5, 2 * W, 2 * W), BF16),
            pltpu.SemaphoreType.DMA((3, 8)),
        ],
        compiler_params=params(48),
        cost_estimate=cost(2 * total * 4 * W * W, total * W * 14, total * W),
    )(counts, arrived, part, edges, *weights, lower, upper, after)


def adding(rows_ref, values_ref, total_ref, also=lambda chunk, values: None):
    span = total_ref.shape[0]
    shift = span.bit_length() - 1
    lists = 4
    height = 256
    zero, one = jnp.zeros((), BF16), jnp.ones((), BF16)
    index = lax.broadcasted_iota(jnp.int32, (height, W), 0).astype(jnp.int16)

    def select(chunk, unused):
        rows = rows_ref[cut(chunk, lists)]
        values = values_ref[cut(chunk, lists * W)]
        also(chunk, values)
        part = columns(rows >> shift).astype(jnp.int16)
        wide = jnp.concatenate(
            [jnp.where(part == jnp.int16(r), values, zero) for r in range(SPLIT)], axis=1
        )
        low = rows & (span - 1)
        across = [
            jnp.concatenate(
                [jnp.broadcast_to(low[i : i + 1], (16, W)).astype(jnp.int16)] * (height // 16),
                axis=0,
            )
            for i in range(lists)
        ]
        hot = [
            jnp.concatenate(
                [jnp.where(row == index + jnp.int16(first), one, zero) for row in across], axis=1
            )
            for first in range(0, span, height)
        ]
        return hot, wide

    def multiply(chunk, given):
        hot, wide = given
        for k, rows in enumerate(hot):
            total_ref[cut(k, height)] += dot(rows, wide)

    return [select, multiply], rows_ref.shape[0] // lists


def received_kernel(
    capacity, counts_ref, edges_ref, rows_ref, values_ref, nodes_ref, inner_ref, outer_ref, first_ref, second_ref, third_ref,
    sums_hbm, prepared_hbm, new_hbm, total_ref, part_ref, weights_ref, new_buf, sem,
):
    total_ref[...] = jnp.zeros_like(total_ref)
    fill(weights_ref, second_ref[...], third_ref[...])
    weights_ref[4] = twice(first_ref[2 * W :])
    edge = outer_ref.shape[0] // 2
    mesh = jnp.concatenate([outer_ref[:edge], inner_ref[...], outer_ref[edge:]], axis=0)
    part_ref[...] = dot(pair(nodes_ref[...]), twice(first_ref[:W])) + dot(
        pair(mesh), twice(first_ref[W : 2 * W])
    )
    span = total_ref.shape[0]
    keep = [
        pltpu.make_async_copy(part_ref, sums_hbm.at[span : 2 * span], sem.at[0]),
        pltpu.make_async_copy(weights_ref, prepared_hbm.at[: weights_ref.shape[0]], sem.at[1]),
    ]
    for copy in keep:
        copy.start()
    slot = lax.broadcasted_iota(jnp.int32, (capacity, W), 0)

    def renew(chunk, values):
        size = values.shape[0]
        here = cut(chunk, size)
        edges = edges_ref[here].astype(F32)
        sent = values.astype(F32)
        peers = size // capacity
        new = [
            jnp.where(
                slot < counts_ref[chunk * peers + p], sent[cut(p, capacity)], edges[cut(p, capacity)]
            )
            for p in range(peers)
        ]
        new_buf[here] = jnp.concatenate(new, axis=0).astype(BF16)
        pltpu.make_async_copy(new_buf.at[here], new_hbm.at[here], sem.at[3]).start()

    pipeline(*adding(rows_ref, values_ref, total_ref, renew))
    keep.append(pltpu.make_async_copy(new_buf, new_hbm, sem.at[3]))
    keep.append(pltpu.make_async_copy(total_ref, sums_hbm.at[:span], sem.at[2]))
    keep[-1].start()
    for copy in keep:
        copy.wait()


def received_sum(
    counts, edges, rows, values, nodes, inner, outer, first, second, third, capacity
):
    span = nodes.shape[0] // SPLIT
    return pl.pallas_call(
        functools.partial(received_kernel, capacity),
        in_specs=[SMEM] + [VMEM] * 9,
        out_specs=[HBM] * 3,
        out_shape=[
            shape(12 * span, F32, SPLIT * W),
            jax.ShapeDtypeStruct((96, 2 * W, 2 * W), BF16),
            shape(values.shape[0]),
        ],
        scratch_shapes=[
            pltpu.VMEM((span, SPLIT * W), F32),
            pltpu.VMEM((span, SPLIT * W), F32),
            pltpu.VMEM((5, 2 * W, 2 * W), BF16),
            pltpu.VMEM(values.shape, BF16),
            pltpu.SemaphoreType.DMA((4,)),
        ],
        compiler_params=params(),
        cost_estimate=cost(2 * values.shape[0] * nodes.shape[0] * W, values.size * 2),
    )(counts, edges, rows, values, nodes, inner, outer, first, second, third)


def node_kernel(
    rows_ref, values_ref, sums_hbm, prepared_hbm, nodes_ref, out_ref, total_ref, sums_ref,
    weights_ref, out_buf, in_sem, sem,
):
    span = total_ref.shape[0]
    sums = Fetch(sums_hbm.at[: 2 * span], sums_ref, in_sem.at[0])
    weights = Fetch(prepared_hbm.at[: weights_ref.shape[0]], weights_ref, in_sem.at[1])
    sums.start()
    weights.start()
    total_ref[...] = jnp.zeros_like(total_ref)
    pipeline(*adding(rows_ref, values_ref, total_ref))
    sums.until(1)
    weights.until(1)
    size = 256

    def first(chunk, unused):
        here = cut(chunk, size)
        world = (total_ref[here] + sums_ref[here]).astype(BF16)
        part = sums_ref[slice(span + chunk * size, span + (chunk + 1) * size)]
        return part + dot(world, weights_ref[4])

    def finish(chunk, given):
        update = normal(given)
        for r in range(SPLIT):
            here = slice(r * span + chunk * size, r * span + (chunk + 1) * size)
            new = nodes_ref[here].astype(F32) + update[:, r * W : (r + 1) * W]
            out_buf[here] = new.astype(BF16)
            pltpu.make_async_copy(out_buf.at[here], out_ref.at[here], sem.at[0]).start()

    pipeline([first] + network(weights_ref) + [finish], span // size)
    pltpu.make_async_copy(out_buf, out_ref, sem.at[0]).wait()


def node_update(rows, values, sums, prepared, nodes):
    span = nodes.shape[0] // SPLIT
    return pl.pallas_call(
        node_kernel,
        in_specs=[VMEM, VMEM, HBM, HBM, VMEM],
        out_specs=HBM,
        out_shape=shape(nodes.shape[0]),
        scratch_shapes=[
            pltpu.VMEM((span, SPLIT * W), F32),
            pltpu.VMEM((2 * span, SPLIT * W), F32),
            pltpu.VMEM((5, 2 * W, 2 * W), BF16),
            pltpu.VMEM(nodes.shape, BF16),
            pltpu.SemaphoreType.DMA((2, 1)),
            pltpu.SemaphoreType.DMA((1,)),
        ],
        compiler_params=params(48),
        cost_estimate=cost(2 * values.shape[0] * nodes.shape[0] * W, values.size * 4, nodes.size),
    )(rows, values, sums, prepared, nodes)


def mesh_stages(
    degree, blocks, table_ref, offset, source_ref, edges_ref, first_ref, weights_ref, target_ref,
    new_buf, new_ref, total_ref, sem,
):
    span = BLOCK + 2 * HALO
    here = degree * BLOCK
    edge_row = lax.broadcasted_iota(jnp.int32, (here, W), 0)
    base = lax.broadcasted_iota(jnp.int32, (here, W), 1) * degree
    near = (edge_row >= base) & (edge_row < base + degree)
    target_ref[...] = jnp.where(near, 1.0, 0.0).astype(BF16)
    down = lax.broadcasted_iota(jnp.int32, (BLOCK, here), 0) * degree
    across = lax.broadcasted_iota(jnp.int32, (BLOCK, here), 1)
    hold = jnp.where((across >= down) & (across < down + degree), 1.0, 0.0).astype(BF16)

    def select(chunk, unused):
        row = blocks[chunk] * BLOCK
        return one_hot(columns(source_ref[blocks[chunk]] - row), span)

    def latents(chunk, hot):
        row = blocks[chunk] * BLOCK - offset
        window = table_ref[row : row + span]
        own = table_ref[row + HALO : row + HALO + BLOCK]
        table = jnp.concatenate(
            [
                jnp.concatenate([window, jnp.zeros_like(window)], axis=1),
                jnp.concatenate([jnp.zeros_like(own), own], axis=1),
            ],
            axis=0,
        )
        return dot(jnp.concatenate([hot, target_ref[...]], axis=1), table).astype(BF16)

    def first(chunk, latent):
        edges = edges_ref[cut(blocks[chunk], here)]
        return pair(dot(jnp.concatenate([edges, latent], axis=1), first_ref[...]))

    def finish(chunk, given):
        edges = edges_ref[cut(blocks[chunk], here)]
        new = (edges.astype(F32) + unpair(normal(given))).astype(BF16)
        new_buf[cut(chunk, here)] = new
        pltpu.make_async_copy(
            new_buf.at[cut(chunk, here)], new_ref.at[cut(blocks[chunk], here)], sem
        ).start()
        return new

    def gather(chunk, new):
        total_ref[cut(chunk, BLOCK)] = dot(hold, new).astype(BF16)

    pipeline([select, latents, first] + network(weights_ref) + [finish, gather], len(blocks))
    pltpu.make_async_copy(new_buf, new_ref.at[: len(blocks) * here], sem).wait()


def inner_kernel(
    degree, blocks, source_ref, edges_ref, nodes_ref, first_ref, second_ref, third_ref, after_ref,
    new_ref, total_ref, token_ref, weights_ref, target_ref, new_buf, sem,
):
    token_ref[...] = jnp.zeros_like(token_ref)
    fill(weights_ref, second_ref[...], third_ref[...])
    mesh_stages(
        degree, blocks, nodes_ref, HALO, source_ref, edges_ref, first_ref, weights_ref, target_ref,
        new_buf, new_ref, total_ref, sem.at[0],
    )


def outer_kernel(
    degree, blocks, source_ref, edges_ref, nodes_ref, first_ref, second_ref, third_ref, after_ref,
    lower_ref, upper_ref, mesh_ref, new_ref, total_ref, weights_ref, target_ref, new_buf, sem,
    table_ref,
):
    count = nodes_ref.shape[0]
    fill(weights_ref, second_ref[...], third_ref[...])
    table_ref[:HALO] = lower_ref[...]
    table_ref[HALO : HALO + count] = nodes_ref[...]
    table_ref[HALO + count :] = upper_ref[...]
    mesh_stages(
        degree, blocks, table_ref, 0, source_ref, edges_ref, first_ref, weights_ref, target_ref,
        new_buf, new_ref, total_ref, sem.at[0],
    )


def mesh_update(kernel, blocks, source, edges, nodes, weights, after, extra=()):
    degree = edges.shape[0] // nodes.shape[0]
    here = degree * BLOCK
    rows = len(blocks) * here
    scratch = [
        pltpu.VMEM((4, 2 * W, 2 * W), BF16),
        pltpu.VMEM((here, W), BF16),
        pltpu.VMEM((rows, W), BF16),
        pltpu.SemaphoreType.DMA((1,)),
    ]
    if extra:
        scratch.append(pltpu.VMEM((nodes.shape[0] + 2 * HALO, W), BF16))
    return pl.pallas_call(
        functools.partial(kernel, degree, blocks),
        in_specs=[VMEM] * 6 + [ANY] + ([VMEM, VMEM, ANY] if extra else []),
        out_specs=[ANY, VMEM] + ([] if extra else [VMEM]),
        out_shape=[shape(edges.shape[0]), shape(len(blocks) * BLOCK)]
        + ([] if extra else [shape(16)]),
        scratch_shapes=scratch,
        input_output_aliases={9: 0} if extra else {},
        compiler_params=params(),
        cost_estimate=cost(2 * rows * 1800 * W, rows * W * 4, rows * W),
    )(source, edges, nodes, *weights, after, *extra)


def shards(
    nodes,
    mesh_edges,
    contact_edges,
    mesh_src,
    halo_rows,
    send_rows,
    partner_rows,
    contact_counts,
    edge_first,
    edge_second,
    edge_third,
    contact_first,
    contact_second,
    contact_third,
    node_first,
    node_second,
    node_third,
):
    axes = ("group", "dom")
    node_count = nodes.shape[0]
    degree = mesh_edges.shape[0] // node_count
    peers, capacity = send_rows.shape
    slots = peers * capacity

    outgoing = gather_rows(send_rows.T, nodes).reshape(peers, capacity, W)
    arrived = lax.all_to_all(outgoing, axes, split_axis=0, concat_axis=0, tiled=True)

    size = lax.axis_size("dom")
    to_lower, to_upper = rim_rows(halo_rows.reshape(-1, W), nodes)
    lower = lax.ppermute(to_upper, "dom", [(i, i + 1) for i in range(size - 1)])
    upper = lax.ppermute(to_lower, "dom", [(i + 1, i) for i in range(size - 1)])

    edges = contact_edges.reshape(slots, W)
    part = partner_part(
        partner_rows.T, nodes, edges, contact_first
    )
    blocks = node_count // BLOCK
    late = 2 * HALO // BLOCK
    inside = tuple(range(late, blocks - late))
    outside = tuple(range(late)) + tuple(range(blocks - late, blocks))
    source = mesh_src.reshape(blocks, degree, BLOCK)
    edge_weights = (edge_first, edge_second, edge_third)
    new_mesh, inner_total, token = mesh_update(
        inner_kernel, inside, source, mesh_edges, nodes, edge_weights, to_lower
    )

    device = lax.axis_index("group") * size + lax.axis_index("dom")
    counts = lax.dynamic_index_in_dim(contact_counts, device, 1, keepdims=False)
    message = contact_rest(
        counts, arrived.reshape(slots, W), part, edges,
        (contact_first, contact_second, contact_third), lower, upper,
        token, capacity
    )
    returned = lax.all_to_all(
        message.reshape(peers, capacity, W), axes, split_axis=0, concat_axis=0, tiled=True
    ).reshape(slots, W)

    new_mesh, outer_total = mesh_update(
        outer_kernel, outside, source, mesh_edges, nodes, edge_weights, message,
        (lower, upper, new_mesh),
    )
    sums, prepared, new_contacts = received_sum(
        counts, edges, partner_rows.reshape(-1, W), message, nodes, inner_total, outer_total,
        node_first, node_second, node_third, capacity,
    )
    new_nodes = node_update(
        send_rows.reshape(-1, W), returned, sums, prepared, nodes
    )
    return (new_nodes, new_mesh, new_contacts.reshape(peers, capacity, W))


def solution(mesh):
    split = P(("group", "dom"))
    in_specs = (split,) * 7 + (P(),) * 10
    return jax.shard_map(
        shards, mesh=mesh, in_specs=in_specs, out_specs=(split,) * 3, check_vma=False
    )
```
